32 devices in a mesh: row: 4 (over y, core), col: 8 (over z, x).
Axes of the slice: x: 2, y: 2, z: 4, core: 2. Of those that a mesh axis runs over, the one named last changes fastest.
Arguments:
- b3c_blocks: bfloat16 [16384, 8, 128], P(('row', 'col')), may hold values from -1.5 to 1.5
- pair_index: int32 [128, 8], P(('row', 'col')), may hold values from 0 to 31, all different within a row
- green_occ: bfloat16 [32, 32], replicated, may hold values from -1 to 1
- green_virt: bfloat16 [128, 128], replicated, may hold values from -0.5 to 0.5
Outputs:
- response: float32 [16384, 4, 8, 512], P('row', None, 'col')
The draws below stay inside these ranges and needn't reach their ends.
Inputs may be any that keep to these rules, and one draw needn't show every extreme that they name: `pair_index`: each row names 8 different values; every value of 0 to 31 is named by some row.
All inputs are finite; a program needn't handle non-finite values.
Results may differ from the reference program's by a relative error of at most 0.0042.
Values may be sent and summed in bfloat16 or wider, within the bound.
No kernel may reach another device: no remote copies, remote signals or barrier semaphores. Data moves between devices by JAX's collectives and lax.ppermute only.
A program may use at most 256 MiB of HBM per device.

```python
import jax
import jax.numpy as jnp
from jax import lax

NRI = 16384
NMU = 32
NNU = 128
NNZ = 8
RBS = 128
NPB = 128
PDEV = 512
N_ROW = 4
N_COL = 8


def block_scale(key, extent, shards, low, high):
    level = 1.0
    for dim, shards_of in shards:
        heights = jax.random.uniform(jax.random.fold_in(jax.random.fold_in(key, 6), dim), (shards_of,), jnp.float32, low / len(shards), high / len(shards))
        level = level * jnp.repeat(jnp.exp(heights), extent[dim] // shards_of).reshape((-1,) + (1,) * (len(extent) - 1 - dim))
    return level


def distinct(stream_key, rows, count, top, lift):
    order = jax.random.permutation(jax.random.fold_in(stream_key, 1), count)
    pull = order
    for power in range(3):
        pull = pull * pull // count
    pull = pull * lift // count
    chance = jax.random.randint(jax.random.fold_in(stream_key, 2), (rows, count), 0, 4096) + pull
    holders = jax.random.permutation(jax.random.fold_in(stream_key, 3), rows)[jnp.arange(count) % rows]
    chance = jnp.where(jnp.arange(rows)[:, None] == holders[None, :], 1 << 14, chance)
    priority = chance * count + jnp.arange(count)
    return lax.top_k(priority.astype(jnp.int32), top)[1].astype(jnp.int32)


def bell_draw(own_key, shape, scale, bound, shards=(), held_as=jnp.bfloat16):
    array = jax.random.normal(own_key, shape, jnp.float32) * scale
    if len(shards) > 0:
        array = block_scale(own_key, shape, shards, -0.22, 0.18) * array
    return jnp.clip(array, min=-bound, max=bound).astype(held_as)


def setup_inputs(seed: int = 0) -> dict:
    key_of = jax.random.split(jax.random.key(seed), 5)
    return {
        "b3c_blocks": bell_draw(key_of[0], (NRI, NNZ, NNU), 0.25, 1.5, ((0, 32),)),
        "pair_index": distinct(key_of[1], NPB, NMU, NNZ, 2048),
        "green_occ": bell_draw(key_of[2], (NMU, NMU), NMU ** -0.5, 1.0),
        "green_virt": bell_draw(key_of[3], (NNU, NNU), NNU ** -0.5, 0.5),
    }


def expand_all(blocks, index):
    onehot = (index[:, :, None] == jnp.arange(NMU, dtype=jnp.int32)[None, None, :]).astype(jnp.float32)
    grouped = blocks.astype(jnp.float32).reshape(NPB, RBS, NNZ, NNU)
    dense = jnp.einsum('bjm,bpjn->bpmn', onehot, grouped)
    return dense.reshape(NRI, NMU, NNU).astype(jnp.bfloat16)


def reference(b3c_blocks, pair_index, green_occ, green_virt):
    tensor = expand_all(b3c_blocks, pair_index)
    half = jnp.einsum('pmn,ns->pms', tensor.astype(jnp.float32), green_virt.astype(jnp.float32)).astype(jnp.bfloat16)
    mixed = jnp.einsum('ml,pms->pls', green_occ.astype(jnp.float32), half.astype(jnp.float32)).astype(jnp.bfloat16)
    left = mixed.reshape(NRI, NMU * NNU)
    right = tensor.reshape(NRI, NMU * NNU)
    chi = jax.lax.dot_general(left, right, (((1,), (1,)), ((), ())), preferred_element_type=jnp.float32)
    return chi.reshape(NRI, N_ROW, N_COL, PDEV)
```

```python
import functools

import jax
import jax.numpy as jnp
import numpy as np
from jax import lax
from jax.experimental import pallas as pl
from jax.experimental.pallas import tpu as pltpu
from jax.sharding import PartitionSpec as P

GROUP = 32
TAIL = 16
SUB = 8
MIB = 1 << 20


def half_kernel(index_ref, raw_ref, virt_ref, *out_refs):
    depth = raw_ref.shape[1]
    blocks, slots = index_ref.shape
    per_piece = blocks // len(out_refs)
    span = raw_ref.shape[0] // len(out_refs)
    row = lax.broadcasted_iota(jnp.int32, (TAIL, depth), 0)
    lane = lax.broadcasted_iota(jnp.int32, (TAIL, depth), 1) % slots
    for n, out_ref in enumerate(out_refs):
        half = jnp.dot(
            raw_ref[n * span : (n + 1) * span, :], virt_ref[...], preferred_element_type=jnp.float32
        )
        out_ref[:span, :] = half.astype(jnp.bfloat16)
        names = jnp.zeros((TAIL, depth), jnp.float32)
        for b in range(per_piece):
            for j in range(slots):
                here = (row == b) & (lane == j)
                names = jnp.where(here, index_ref[n * per_piece + b, j].astype(jnp.float32), names)
        out_ref[span:, :] = names.astype(jnp.bfloat16)


def make_half(raw, pair_index, green_virt, pieces):
    span, depth = raw.shape[0] // pieces, raw.shape[1]
    vmem = pl.BlockSpec(memory_space=pltpu.VMEM)
    return pl.pallas_call(
        half_kernel,
        in_specs=[pl.BlockSpec(memory_space=pltpu.SMEM), vmem, vmem],
        out_specs=[vmem] * pieces,
        out_shape=[jax.ShapeDtypeStruct((span + TAIL, depth), jnp.bfloat16)] * pieces,
        name="half",
    )(pair_index, raw, green_virt)


def turn_kernel(raw_ref, out_ref):
    _, slots, depth, rows = out_ref.shape
    span = GROUP * slots
    to = lax.broadcasted_iota(jnp.int32, (span, span), 0)
    at = lax.broadcasted_iota(jnp.int32, (span, span), 1)
    same = (to // GROUP == at % slots) & (to % GROUP == at // slots)
    move = jnp.where(same, 1.0, 0.0).astype(jnp.bfloat16)
    parts = [
        jnp.dot(move, raw_ref[g * span : (g + 1) * span, :], preferred_element_type=jnp.float32)
        for g in range(rows // GROUP)
    ]
    for j in range(slots):
        slab = jnp.concatenate([part[j * GROUP : (j + 1) * GROUP, :] for part in parts], axis=0)
        out_ref[0, j] = slab.T.astype(jnp.bfloat16)


def make_turn(raw, blocks, slots, rows):
    depth = raw.shape[1]
    return pl.pallas_call(
        turn_kernel,
        grid=(blocks,),
        in_specs=[pl.BlockSpec((rows * slots, depth), lambda b: (b, 0))],
        out_specs=pl.BlockSpec((1, slots, depth, rows), lambda b: (b, 0, 0, 0)),
        out_shape=jax.ShapeDtypeStruct((blocks, slots, depth, rows), jnp.bfloat16),
        name="turn",
    )(raw)


def panel_kernel(place_ref, index_ref, occ_ref, *rest, pieces, owners, rows, first_place):
    piece_refs = rest[:pieces]
    turned_refs = rest[pieces : pieces + owners]
    out_ref, half_buf, turned_buf, mixed_buf, out_buf, in_sem, turned_sem, out_sem = rest[-8:]
    width, total, depth = mixed_buf.shape
    blocks, slots = turned_buf.shape[1:3]
    span = half_buf.shape[1] - TAIL
    per_piece = span // (rows * slots)
    height = per_piece * rows
    groups = out_ref.shape[1]
    loads = [
        pltpu.make_async_copy(piece_refs[n], half_buf.at[n], in_sem.at[n]) for n in range(pieces)
    ]
    turned = [
        pltpu.make_async_copy(turned_refs[n], turned_buf.at[n], turned_sem.at[n])
        for n in range(owners)
    ]
    for load in loads + turned:
        load.start()
    wide = GROUP * slots
    level = lax.broadcasted_iota(jnp.int32, (width, wide), 0).astype(jnp.float32)
    to = lax.broadcasted_iota(jnp.int32, (width * GROUP, wide), 0) % GROUP
    at = lax.broadcasted_iota(jnp.int32, (width * GROUP, wide), 1) // slots
    same = to == at
    for n in range(pieces):
        loads[n].wait()
        names = half_buf[n, span:, :].astype(jnp.float32)
        for b in range(per_piece):
            name = jnp.concatenate([names[b : b + 1, :]] * (wide // depth), axis=1)
            named = jnp.where(level == name, 1.0, 0.0).astype(jnp.bfloat16)
            picked = lax.dot_general(
                occ_ref[...], named, (((0,), (0,)), ((), ())), preferred_element_type=jnp.float32
            )
            mix = jnp.broadcast_to(picked[:, None, :], (width, GROUP, wide))
            mix = jnp.where(same, mix.reshape(width * GROUP, wide), 0.0).astype(jnp.bfloat16)
            base = b * rows * slots
            for g in range(0, rows // GROUP, 2):
                right = jnp.concatenate(
                    [
                        half_buf[n, base + (g + e) * wide : base + (g + e + 1) * wide, :]
                        for e in range(2)
                    ],
                    axis=1,
                )
                part = jnp.dot(mix, right, preferred_element_type=jnp.float32).astype(jnp.bfloat16)
                for e in range(2):
                    first = n * height + b * rows + (g + e) * GROUP
                    mixed_buf[:, first : first + GROUP, :] = part[
                        :, e * depth : (e + 1) * depth
                    ].reshape(width, GROUP, depth)
    for load in turned:
        load.wait()
    stores = []
    for group in range(groups):
        flat = out_buf.at[group].reshape(total * SUB, depth)

        def column(k, carry):
            tile = group * SUB + k
            owner = place_ref[tile // blocks]
            block = tile % blocks
            left = jnp.concatenate(
                [mixed_buf[index_ref[owner * blocks + block, j]] for j in range(slots)], axis=1
            )
            right = turned_buf[owner, block].reshape(slots * depth, rows)
            flat[pl.ds(k, total, stride=SUB), :] = jnp.dot(
                left, right, preferred_element_type=jnp.float32
            )
            return carry

        lax.fori_loop(0, SUB, column, 0, unroll=True)
        for n in range(pieces):
            first = pl.multiple_of(place_ref[first_place + n] * height, height)
            store = pltpu.make_async_copy(
                out_buf.at[group, pl.ds(n * height, height)],
                out_ref.at[pl.ds(first, height), group],
                out_sem.at[group, n],
            )
            store.start()
            stores.append(store)
    for store in stores:
        store.wait()


def make_panel(place, first_place, index, green_occ, pieces, turned, rows, total, before):
    span, depth = pieces[0].shape[0] - TAIL, pieces[0].shape[1]
    blocks, slots = turned[0].shape[:2]
    owners = len(turned)
    width = green_occ.shape[0]
    height = span // slots
    here = len(pieces) * height
    groups = owners * blocks // SUB
    extra = [] if before is None else [before]
    anywhere = pl.BlockSpec(memory_space=pl.ANY)
    smem = pl.BlockSpec(memory_space=pltpu.SMEM)
    columns = owners * blocks * rows
    return pl.pallas_call(
        functools.partial(
            panel_kernel, pieces=len(pieces), owners=owners, rows=rows, first_place=first_place
        ),
        in_specs=[smem, smem, pl.BlockSpec(memory_space=pltpu.VMEM)]
        + [anywhere] * (len(pieces) + owners + len(extra)),
        out_specs=anywhere,
        out_shape=jax.ShapeDtypeStruct((total, groups, SUB, depth), jnp.float32),
        scratch_shapes=[
            pltpu.VMEM((len(pieces), span + TAIL, depth), jnp.bfloat16),
            pltpu.VMEM((owners, blocks, slots, depth, rows), jnp.bfloat16),
            pltpu.VMEM((width, here, depth), jnp.bfloat16),
            pltpu.VMEM((groups, here, SUB, depth), jnp.float32),
            pltpu.SemaphoreType.DMA((len(pieces),)),
            pltpu.SemaphoreType.DMA((owners,)),
            pltpu.SemaphoreType.DMA((groups, len(pieces))),
        ],
        input_output_aliases={3 + len(pieces) + owners: 0} if extra else {},
        compiler_params=pltpu.CompilerParams(vmem_limit_bytes=56 * MIB),
        cost_estimate=pl.CostEstimate(
            flops=2 * here * columns * slots * depth * 2,
            bytes_accessed=4 * here * columns,
            transcendentals=0,
        ),
        name="panel",
    )(place, index, green_occ, *pieces, *turned, *extra)


def cycle(count):
    return list(range(0, count, 2)) + list(range(1, count, 2))[::-1]


def ring(count):
    walk = cycle(count)
    return [
        (2 * walk[n] + e, 2 * walk[(n + 1) % count] + e) for n in range(count) for e in range(2)
    ]


def swap(count):
    return [(n, n ^ 1) for n in range(count)]


def behind(index, steps, count):
    walk = cycle(count)
    return 2 * walk[(walk.index(index // 2) - steps) % count] + index % 2


def on_device(b3c_blocks, pair_index, green_occ, green_virt):
    per_device, slots, depth = b3c_blocks.shape
    blocks = pair_index.shape[0]
    rows = per_device // blocks
    n_row, n_col = lax.axis_size("row"), lax.axis_size("col")
    row, col = lax.axis_index("row"), lax.axis_index("col")
    outer, outer_row = n_col // 2, n_row // 2
    cuts = 2 if blocks % 2 == 0 else 1
    raw = b3c_blocks.reshape(per_device * slots, depth)

    turn_col = functools.partial(lax.ppermute, axis_name="col", perm=ring(outer))
    swap_col = functools.partial(lax.ppermute, axis_name="col", perm=swap(n_col))
    turn_row = functools.partial(lax.ppermute, axis_name="row", perm=ring(outer_row))
    swap_row = functools.partial(lax.ppermute, axis_name="row", perm=swap(n_row))

    pairs = jnp.concatenate([pair_index, swap_row(pair_index)], axis=0)
    names = [pairs]
    for _ in range(outer_row - 1):
        names.append(turn_row(names[-1]))
    index = jnp.concatenate(names, axis=0)
    turned = [make_turn(raw, blocks, slots, rows)]
    for _ in range(outer_row - 1):
        turned.append(turn_row(turned[-1]))
    turned = [a for t in turned for a in (t, swap_row(t))]

    held = {}
    for n, piece in enumerate(make_half(raw, pair_index, green_virt, cuts)):
        held[0, 0, n] = piece
    for n in range(cuts):
        held[0, 1, n] = swap_col(held[0, 0, n])
    for k in range(1, outer):
        for n in range(cuts):
            held[k, 0, n] = turn_col(held[k - 1, 0, n])
            if k == 1 and n == cuts - 1 and cuts > 1:
                held[k, 1, n] = turn_col(held[0, 1, n])
            else:
                held[k, 1, n] = swap_col(held[k, 0, n])
    order = [[(0, 0, n) for n in range(cuts)]]
    left = [key for key in held if key[:2] != (0, 0)]
    if outer == 4 and cuts == 2:
        order += [
            [(1, 0, 0), (0, 1, 0)],
            [(1, 0, 1), (0, 1, 1)],
            [(2, 0, 0), (1, 1, 0)],
            [(2, 0, 1), (2, 1, 0)],
            [(3, 0, 0), (2, 1, 1)],
            [(3, 0, 1), (3, 1, 0)],
            [(1, 1, 1), (3, 1, 1)],
        ]
    else:
        order += [[key] for key in left]

    table = np.zeros((n_row, n_col, n_row + n_col * cuts), np.int32)
    for r in range(n_row):
        for k in range(outer_row):
            for e in range(2):
                table[r, :, behind(r, k, outer_row) ^ e] = 2 * k + e
    for c in range(n_col):
        for n, (k, e, cut) in enumerate(key for call in order for key in call):
            table[:, c, n_row + n] = (behind(c, k, outer) ^ e) * cuts + cut
    place = lax.dynamic_index_in_dim(
        jnp.asarray(table).reshape(n_row * n_col, -1), row * n_col + col, 0, keepdims=False
    )
    panel, first_place = None, n_row
    for call in order:
        pieces = [held[key] for key in call]
        panel = make_panel(
            place, first_place, index, green_occ, pieces, turned, rows, n_col * per_device, panel
        )
        first_place += len(call)
    return panel.reshape(n_col * per_device, n_row, 1, per_device)


def solution(mesh):
    return jax.shard_map(
        on_device,
        mesh=mesh,
        in_specs=(P(("row", "col"), None, None), P(("row", "col"), None), P(), P()),
        out_specs=P("row", None, "col", None),
        check_vma=False,
    )
```

```python
import functools

import jax
import jax.numpy as jnp
import numpy as np
from jax import lax
from jax.experimental import pallas as pl
from jax.experimental.pallas import tpu as pltpu
from jax.sharding import PartitionSpec as P

GROUP = 32
TAIL = 16
SUB = 8
MIB = 1 << 20
VMEM_LIMIT = 62


def names_of(index_ref, first, count, lanes):
    slots = index_ref.shape[1]
    row = lax.broadcasted_iota(jnp.int32, (TAIL, lanes), 0)
    lane = lax.broadcasted_iota(jnp.int32, (TAIL, lanes), 1) % slots
    names = jnp.zeros((TAIL, lanes), jnp.float32)
    for b in range(count):
        for j in range(slots):
            here = (row == b) & (lane == j)
            names = jnp.where(here, index_ref[first + b, j].astype(jnp.float32), names)
    return names.astype(jnp.bfloat16)


def half_kernel(index_ref, raw_ref, virt_ref, *out_refs):
    depth = raw_ref.shape[1]
    blocks = index_ref.shape[0]
    per_piece = blocks // len(out_refs)
    span = raw_ref.shape[0] // len(out_refs)
    for n, out_ref in enumerate(out_refs):
        half = jnp.dot(
            raw_ref[n * span : (n + 1) * span, :], virt_ref[...], preferred_element_type=jnp.float32
        )
        out_ref[:span, :] = half.astype(jnp.bfloat16)
        out_ref[span:, :] = names_of(index_ref, n * per_piece, per_piece, depth)


def make_half(raw, pair_index, green_virt, pieces):
    span, depth = raw.shape[0] // pieces, raw.shape[1]
    vmem = pl.BlockSpec(memory_space=pltpu.VMEM)
    return pl.pallas_call(
        half_kernel,
        in_specs=[pl.BlockSpec(memory_space=pltpu.SMEM), vmem, vmem],
        out_specs=[vmem] * pieces,
        out_shape=[jax.ShapeDtypeStruct((span + TAIL, depth), jnp.bfloat16)] * pieces,
        name="half",
    )(pair_index, raw, green_virt)


def turn_kernel(raw_ref, out_ref, *, blocks, slots, rows):
    depth = raw_ref.shape[1]
    span = GROUP * slots
    to = lax.broadcasted_iota(jnp.int32, (span, span), 0)
    at = lax.broadcasted_iota(jnp.int32, (span, span), 1)
    same = (to // GROUP == at % slots) & (to % GROUP == at // slots)
    move = jnp.where(same, 1.0, 0.0).astype(jnp.bfloat16)
    for b in range(blocks):
        base = b * rows * slots
        parts = [
            jnp.dot(
                move,
                raw_ref[base + g * span : base + (g + 1) * span, :],
                preferred_element_type=jnp.float32,
            )
            for g in range(rows // GROUP)
        ]
        for j in range(slots):
            slab = jnp.concatenate([part[j * GROUP : (j + 1) * GROUP, :] for part in parts], axis=0)
            first = (b * slots + j) * depth
            out_ref[first : first + depth, :] = slab.T.astype(jnp.bfloat16)


def make_turn(raw, blocks, slots, rows):
    depth = raw.shape[1]
    vmem = pl.BlockSpec(memory_space=pltpu.VMEM)
    return pl.pallas_call(
        functools.partial(turn_kernel, blocks=blocks, slots=slots, rows=rows),
        in_specs=[vmem],
        out_specs=vmem,
        out_shape=jax.ShapeDtypeStruct((blocks * slots * depth, rows), jnp.bfloat16),
        name="turn",
    )(raw)


def mix_pieces(occ_ref, half_buf, mixed_buf, loads, rows, slots):
    width, _, depth = mixed_buf.shape
    span = half_buf.shape[1] - TAIL
    per_piece = span // (rows * slots)
    wide = GROUP * slots
    level = lax.broadcasted_iota(jnp.int32, (width, wide), 0).astype(jnp.float32)
    to = lax.broadcasted_iota(jnp.int32, (width * GROUP, wide), 0) % GROUP
    at = lax.broadcasted_iota(jnp.int32, (width * GROUP, wide), 1) // slots
    same = to == at
    for n, load in enumerate(loads):
        load.wait()
        names = half_buf[n, span:, :].astype(jnp.float32)
        for b in range(per_piece):
            name = jnp.concatenate([names[b : b + 1, :]] * (wide // depth), axis=1)
            named = jnp.where(level == name, 1.0, 0.0).astype(jnp.bfloat16)
            picked = lax.dot_general(
                occ_ref[...], named, (((0,), (0,)), ((), ())), preferred_element_type=jnp.float32
            )
            mix = jnp.broadcast_to(picked[:, None, :], (width, GROUP, wide))
            mix = jnp.where(same, mix.reshape(width * GROUP, wide), 0.0).astype(jnp.bfloat16)
            base = b * rows * slots
            for g in range(0, rows // GROUP, 2):
                right = jnp.concatenate(
                    [
                        half_buf[n, base + (g + e) * wide : base + (g + e + 1) * wide, :]
                        for e in range(2)
                    ],
                    axis=1,
                )
                part = jnp.dot(mix, right, preferred_element_type=jnp.float32).astype(jnp.bfloat16)
                for e in range(2):
                    first = (n * per_piece + b) * rows + (g + e) * GROUP
                    mixed_buf[:, first : first + GROUP, :] = part[
                        :, e * depth : (e + 1) * depth
                    ].reshape(width, GROUP, depth)


def panel_kernel(place_ref, occ_ref, *rest, plan):
    (units, kept, indices, owners, extra, keep, blocks, slots, first_owner, first_group) = plan
    rest = list(rest)
    take = lambda count: [rest.pop(0) for _ in range(count)]
    index_refs = take(indices)
    unit_refs = [take(1 if kept else len(unit)) for unit in units]
    turned_refs = take(owners)
    take(extra)
    out_ref, token_ref = take(2)
    token_ref[0] = 0
    keep_refs = take(len(units) if keep else 0)
    half_buf, turned_buf, mixed_buf, out_buf, in_sem, turned_sem, out_sem, keep_sem = rest
    here, depth = mixed_buf.shape[2:]
    rows = turned_buf.shape[2]
    height = here // len(units[0])
    groups = out_buf.shape[1]
    loads = []
    for u, refs in enumerate(unit_refs):
        loads.append([])
        for n, ref in enumerate(refs):
            to = mixed_buf.at[u] if kept else half_buf.at[u, n]
            loads[u].append(pltpu.make_async_copy(ref, to, in_sem.at[u, n]))
    turned = [
        pltpu.make_async_copy(turned_refs[n], turned_buf.at[n], turned_sem.at[n])
        for n in range(owners)
    ]
    for load in [load for unit in loads for load in unit] + turned:
        load.start()
    stores = []
    for u, unit in enumerate(units):
        if kept:
            loads[u][0].wait()
        else:
            mix_pieces(occ_ref, half_buf.at[u], mixed_buf.at[u], loads[u], rows, slots)
        if keep:
            store = pltpu.make_async_copy(mixed_buf.at[u], keep_refs[u], keep_sem.at[u])
            store.start()
            stores.append(store)
        if u == 0:
            for load in turned:
                load.wait()
        for g in range(groups):
            group = place_ref[first_group + g]
            flat = out_buf.at[u, g].reshape(here * SUB, depth)
            index_ref = index_refs[g * indices // groups]

            def column(k, carry):
                tile = group * SUB + k
                owner = place_ref[tile // blocks] - first_owner
                block = tile % blocks
                named = lax.rem(owner, owners // indices) * blocks + block
                left = jnp.concatenate(
                    [mixed_buf[u, index_ref[named, j]] for j in range(slots)], axis=1
                )
                first = pl.multiple_of(block * (slots * depth), slots * depth)
                right = turned_buf[owner, pl.ds(first, slots * depth), :]
                flat[pl.ds(k, here, stride=SUB), :] = jnp.dot(
                    left, right, preferred_element_type=jnp.float32
                )
                return carry

            lax.fori_loop(0, SUB, column, 0, unroll=True)
            for n, at in enumerate(unit):
                first = pl.multiple_of(place_ref[at] * height, height)
                store = pltpu.make_async_copy(
                    out_buf.at[u, g, pl.ds(n * height, height)],
                    out_ref.at[pl.ds(first, height), group],
                    out_sem.at[u, g, n],
                )
                store.start()
                stores.append(store)
    for store in stores:
        store.wait()


def make_panel(
    place, green_occ, index, units, at, turned, first_owner, first_group, sizes, before, keep, kept
):
    blocks, slots, width, total, groups, height = sizes
    depth, rows = turned[0].shape[0] // (blocks * slots), turned[0].shape[1]
    owners = len(turned)
    here = len(at[0]) * height
    own_groups = owners * blocks // SUB
    extra = [] if before is None else [before]
    flat = [a for unit in units for a in unit]
    plan = (
        at, kept, len(index), owners, len(extra), keep, blocks, slots, first_owner, first_group
    )
    anywhere = pl.BlockSpec(memory_space=pl.ANY)
    smem = pl.BlockSpec(memory_space=pltpu.SMEM)
    mixed = jax.ShapeDtypeStruct((width, here, depth), jnp.bfloat16)
    out = jax.ShapeDtypeStruct((total, groups, SUB, depth), jnp.float32)
    count = len(units)
    return pl.pallas_call(
        functools.partial(panel_kernel, plan=plan),
        in_specs=[smem, pl.BlockSpec(memory_space=pltpu.VMEM)]
        + [smem] * len(index)
        + [anywhere] * (len(flat) + owners + len(extra)),
        out_specs=[anywhere, smem] + [anywhere] * (count * keep),
        out_shape=[out, jax.ShapeDtypeStruct((1,), jnp.int32)] + [mixed] * (count * keep),
        scratch_shapes=[
            pltpu.VMEM((count, len(at[0]), height * slots + TAIL, depth), jnp.bfloat16),
            pltpu.VMEM((owners, blocks * slots * depth, rows), jnp.bfloat16),
            pltpu.VMEM((count, width, here, depth), jnp.bfloat16),
            pltpu.VMEM((count, own_groups, here, SUB, depth), jnp.float32),
            pltpu.SemaphoreType.DMA((count, len(at[0]))),
            pltpu.SemaphoreType.DMA((owners,)),
            pltpu.SemaphoreType.DMA((count, own_groups, len(at[0]))),
            pltpu.SemaphoreType.DMA((count,)),
        ],
        input_output_aliases={2 + len(index) + len(flat) + owners: 0} if extra else {},
        compiler_params=pltpu.CompilerParams(vmem_limit_bytes=VMEM_LIMIT * MIB),
        cost_estimate=pl.CostEstimate(
            flops=12 * count * here * owners * blocks * rows * slots * depth,
            bytes_accessed=4 * count * here * owners * blocks * rows,
            transcendentals=0,
        ),
        name="panel",
    )(place, green_occ, *index, *flat, *turned, *extra)


def touch_kernel(token_ref, array_ref, out_ref):
    pass


def after(token, array):
    anywhere = pl.BlockSpec(memory_space=pl.ANY)
    return pl.pallas_call(
        touch_kernel,
        in_specs=[pl.BlockSpec(memory_space=pltpu.SMEM), anywhere],
        out_specs=anywhere,
        out_shape=jax.ShapeDtypeStruct(array.shape, array.dtype),
        input_output_aliases={1: 0},
        name="after",
    )(token, array)


def cycle(count):
    return list(range(0, count, 2)) + list(range(1, count, 2))[::-1]


def ring(count):
    walk = cycle(count)
    return [
        (2 * walk[n] + e, 2 * walk[(n + 1) % count] + e) for n in range(count) for e in range(2)
    ]


def swap(count):
    return [(n, n ^ 1) for n in range(count)]


def behind(index, steps, count):
    walk = cycle(count)
    return 2 * walk[(walk.index(index // 2) - steps) % count] + index % 2


def on_device(b3c_blocks, pair_index, green_occ, green_virt):
    per_device, slots, depth = b3c_blocks.shape
    blocks = pair_index.shape[0]
    rows = per_device // blocks
    n_row, n_col = lax.axis_size("row"), lax.axis_size("col")
    row, col = lax.axis_index("row"), lax.axis_index("col")
    outer, outer_row = n_col // 2, n_row // 2
    cuts = 2 if blocks % 2 == 0 else 1
    total = n_col * per_device
    groups = n_row * blocks // SUB
    split = 2 * blocks == SUB
    sizes = (blocks, slots, green_occ.shape[0], total, groups, per_device // cuts)
    raw = b3c_blocks.reshape(per_device * slots, depth)

    turn_col = functools.partial(lax.ppermute, axis_name="col", perm=ring(outer))
    swap_col = functools.partial(lax.ppermute, axis_name="col", perm=swap(n_col))
    turn_row = functools.partial(lax.ppermute, axis_name="row", perm=ring(outer_row))
    swap_row = functools.partial(lax.ppermute, axis_name="row", perm=swap(n_row))

    every = [(k, e, n) for k in range(outer) for e in range(2) for n in range(cuts)]
    number = {key: n_row + groups + n for n, key in enumerate(every)}
    table = np.zeros((n_row, n_col, n_row + groups + len(every)), np.int32)
    for r in range(n_row):
        for k in range(outer_row):
            for e in range(2):
                table[r, :, behind(r, k, outer_row) ^ e] = 2 * k + e
            if split:
                table[r, :, n_row + k] = behind(r, k, outer_row) // 2
    if not split:
        table[:, :, n_row : n_row + groups] = np.arange(groups)
    for c in range(n_col):
        for key in every:
            k, e, cut = key
            table[:, c, number[key]] = (behind(c, k, outer) ^ e) * cuts + cut
    place = lax.dynamic_index_in_dim(
        jnp.asarray(table).reshape(n_row * n_col, -1), row * n_col + col, 0, keepdims=False
    )

    held, kept, state = {}, {}, {"panel": None}
    for n, piece in enumerate(make_half(raw, pair_index, green_virt, cuts)):
        held[0, 0, n] = piece
    turned = [make_turn(raw, blocks, slots, rows)]
    for k in range(outer_row - 1):
        turned.append(turn_row(turned[-1]))
    turned = [a for t in turned for a in (t, swap_row(t))]
    index = [jnp.concatenate([pair_index, swap_row(pair_index)], axis=0)]
    for k in range(outer_row - 1):
        index.append(turn_row(index[-1]))
    if not split:
        index = [jnp.concatenate(index, axis=0)]

    def step(k, n):
        held[k, 0, n] = turn_col(held[k - 1, 0, n])

    def cross(k, n):
        held[k, 1, n] = swap_col(held[k, 0, n])

    def panel(units, first, count, keep=False, reuse=False):
        at = [[number[key] for key in unit] for unit in units]
        data = [[kept[tuple(unit)]] if reuse else [held[key] for key in unit] for unit in units]
        here = index[first // 2 : (first + count) // 2] if split else index
        first_group = n_row + (first // 2 if split else 0)
        state["panel"], token, *mixed = make_panel(
            place, green_occ, here, data, at, turned[first : first + count], first, first_group,
            sizes, state["panel"], keep, reuse,
        )
        for unit, array in zip(units, mixed):
            kept[tuple(unit)] = array
        return token

    if outer == 4 and cuts == 2 and split and outer_row == 2:
        A, B = 0, 1
        for n in range(2):
            step(1, n)
            cross(0, n)
            step(2, n)
        cross(1, A)
        early = [
            [(0, 0, A), (0, 0, B)], [(1, 0, A), (0, 1, A)], [(1, 0, B), (0, 1, B)]
        ]
        for unit in early:
            token = panel([unit], 0, 2, keep=True)
        step(3, A)
        cross(2, A)
        token = panel(early, 2, 2, reuse=True)
        held[2, 0, B] = after(token, held[2, 0, B])
        step(3, B)
        cross(2, B)
        held[1, 1, B] = turn_col(held[0, 1, B])
        token = panel([[(2, 0, A), (1, 1, A)]], 0, 4)
        held[3, 0, A] = after(token, held[3, 0, A])
        cross(3, A)
        token = panel([[(2, 0, B), (2, 1, A)]], 0, 4)
        held[3, 0, B] = after(token, held[3, 0, B])
        cross(3, B)
        panel([[(3, 0, A), (2, 1, B)]], 0, 4)
        panel([[(3, 0, B), (3, 1, A)]], 0, 4)
        panel([[(1, 1, B), (3, 1, B)]], 0, 4)
    else:
        for k in range(outer):
            for n in range(cuts):
                if k > 0:
                    step(k, n)
                cross(k, n)
        for key in every:
            panel([[key]], 0, n_row)
    return state["panel"].reshape(total, n_row, 1, per_device)


def solution(mesh):
    return jax.shard_map(
        on_device,
        mesh=mesh,
        in_specs=(P(("row", "col"), None, None), P(("row", "col"), None), P(), P()),
        out_specs=P("row", None, "col", None),
        check_vma=False,
    )
```

```python
import functools

import jax
import jax.numpy as jnp
import numpy as np
from jax import lax
from jax.experimental import pallas as pl
from jax.experimental.pallas import tpu as pltpu
from jax.sharding import PartitionSpec as P

GROUP = 32
TAIL = 16
SUB = 8
MIB = 1 << 20
VMEM_LIMIT = 36


def names_of(index_ref, first, count, lanes):
    slots = index_ref.shape[1]
    row = lax.broadcasted_iota(jnp.int32, (TAIL, lanes), 0)
    lane = lax.broadcasted_iota(jnp.int32, (TAIL, lanes), 1) % slots
    names = jnp.zeros((TAIL, lanes), jnp.float32)
    for b in range(count):
        for j in range(slots):
            here = (row == b) & (lane == j)
            names = jnp.where(here, index_ref[first + b, j].astype(jnp.float32), names)
    return names.astype(jnp.bfloat16)


def prepare_kernel(index_ref, raw_ref, virt_ref, *out_refs):
    *half_refs, turned_ref = out_refs
    depth = raw_ref.shape[1]
    blocks, slots = index_ref.shape
    rows = turned_ref.shape[1]
    per_piece = blocks // len(half_refs)
    span = raw_ref.shape[0] // len(half_refs)
    for n, half_ref in enumerate(half_refs):
        half = jnp.dot(
            raw_ref[n * span : (n + 1) * span, :], virt_ref[...], preferred_element_type=jnp.float32
        )
        half_ref[:span, :] = half.astype(jnp.bfloat16)
        half_ref[span:, :] = names_of(index_ref, n * per_piece, per_piece, depth)
    span = GROUP * slots
    to = lax.broadcasted_iota(jnp.int32, (span, span), 0)
    at = lax.broadcasted_iota(jnp.int32, (span, span), 1)
    same = (to // GROUP == at % slots) & (to % GROUP == at // slots)
    move = jnp.where(same, 1.0, 0.0).astype(jnp.bfloat16)
    for b in range(blocks):
        base = b * rows * slots
        parts = [
            jnp.dot(
                move,
                raw_ref[base + g * span : base + (g + 1) * span, :],
                preferred_element_type=jnp.float32,
            )
            for g in range(rows // GROUP)
        ]
        for j in range(slots):
            slab = jnp.concatenate([part[j * GROUP : (j + 1) * GROUP, :] for part in parts], axis=0)
            first = (b * slots + j) * depth
            turned_ref[first : first + depth, :] = slab.T.astype(jnp.bfloat16)


def prepare(raw, pair_index, green_virt, pieces, rows):
    span, depth = raw.shape[0] // pieces, raw.shape[1]
    blocks, slots = pair_index.shape
    vmem = pl.BlockSpec(memory_space=pltpu.VMEM)
    *halves, turned = pl.pallas_call(
        prepare_kernel,
        in_specs=[pl.BlockSpec(memory_space=pltpu.SMEM), vmem, vmem],
        out_specs=[vmem] * (pieces + 1),
        out_shape=[jax.ShapeDtypeStruct((span + TAIL, depth), jnp.bfloat16)] * pieces
        + [jax.ShapeDtypeStruct((blocks * slots * depth, rows), jnp.bfloat16)],
        name="prepare",
    )(pair_index, raw, green_virt)
    return halves, turned


def mix_pieces(occ_ref, piece_refs, mixed_ref, rows, slots):
    width, _, depth = mixed_ref.shape
    span = piece_refs[0].shape[0] - TAIL
    per_piece = span // (rows * slots)
    wide = GROUP * slots
    level = lax.broadcasted_iota(jnp.int32, (width, wide), 0).astype(jnp.float32)
    to = lax.broadcasted_iota(jnp.int32, (width * GROUP, wide), 0) % GROUP
    at = lax.broadcasted_iota(jnp.int32, (width * GROUP, wide), 1) // slots
    same = to == at
    for n, piece_ref in enumerate(piece_refs):
        names = piece_ref[span:, :].astype(jnp.float32)
        for b in range(per_piece):
            name = jnp.concatenate([names[b : b + 1, :]] * (wide // depth), axis=1)
            named = jnp.where(level == name, 1.0, 0.0).astype(jnp.bfloat16)
            picked = lax.dot_general(
                occ_ref[...], named, (((0,), (0,)), ((), ())), preferred_element_type=jnp.float32
            )
            mix = jnp.broadcast_to(picked[:, None, :], (width, GROUP, wide))
            mix = jnp.where(same, mix.reshape(width * GROUP, wide), 0.0).astype(jnp.bfloat16)
            base = b * rows * slots
            for g in range(0, rows // GROUP, 2):
                right = jnp.concatenate(
                    [
                        piece_ref[base + (g + e) * wide : base + (g + e + 1) * wide, :]
                        for e in range(2)
                    ],
                    axis=1,
                )
                part = jnp.dot(mix, right, preferred_element_type=jnp.float32).astype(jnp.bfloat16)
                for e in range(2):
                    first = (n * per_piece + b) * rows + (g + e) * GROUP
                    mixed_ref[:, first : first + GROUP, :] = part[
                        :, e * depth : (e + 1) * depth
                    ].reshape(width, GROUP, depth)


def panel_kernel(place_ref, occ_ref, *rest, plan):
    (units, kept, owners, extra, keep, token, blocks, slots, first_owner) = plan
    rest = list(rest)
    take = lambda count: [rest.pop(0) for _ in range(count)]
    index_refs = take(owners // 2)
    unit_refs = [take(1 if kept else len(unit)) for unit in units]
    turned_refs = take(owners)
    take(extra)
    out_ref = rest.pop(0)
    for token_ref in take(token):
        token_ref[0] = 0
    mixed_refs = [refs[0] for refs in unit_refs] if kept else take(len(units))
    out_buf, out_sem = rest
    here, depth = mixed_refs[0].shape[1:]
    height = here // len(units[0])
    per_group = SUB // blocks
    stores = []
    here_too = place_ref[0] >= 0
    for u, unit in enumerate(units):
        mixed_ref = mixed_refs[u]
        if not kept:

            @pl.when(here_too)
            def _():
                rows = turned_refs[0].shape[1]
                mix_pieces(occ_ref, unit_refs[u], mixed_ref, rows, slots)

        for g in range(owners // per_group):
            flat = out_buf.at[u, g].reshape(here * SUB, depth)
            tile = place_ref[first_owner + g * per_group] * blocks

            @pl.when(here_too)
            def _():
                for n in range(g * per_group, (g + 1) * per_group):
                    first = lax.rem(place_ref[first_owner + n] * blocks, SUB)
                    for b in range(blocks):
                        left = jnp.concatenate(
                            [
                                mixed_ref[index_refs[n // 2][n % 2 * blocks + b, j]]
                                for j in range(slots)
                            ],
                            axis=1,
                        )
                        right = turned_refs[n][b * slots * depth : (b + 1) * slots * depth, :]
                        flat[pl.ds(first + b, here, stride=SUB), :] = jnp.dot(
                            left, right, preferred_element_type=jnp.float32
                        )

            for n, at in enumerate(unit):
                first = pl.multiple_of(place_ref[at] * height, height)
                store = pltpu.make_async_copy(
                    out_buf.at[u, g, pl.ds(n * height, height)],
                    out_ref.at[pl.ds(first, height), tile // SUB],
                    out_sem.at[u, g, n],
                )
                store.start()
                stores.append(store)
    for store in stores:
        store.wait()


def make_panel(
    place, green_occ, index, units, at, turned, first_owner, sizes, before, keep, kept, token
):
    blocks, slots, width, total, groups, height = sizes
    depth, rows = turned[0].shape[0] // (blocks * slots), turned[0].shape[1]
    owners = len(turned)
    here = len(at[0]) * height
    own_groups = owners * blocks // SUB
    extra = [] if before is None else [before]
    flat = [a for unit in units for a in unit]
    plan = (at, kept, owners, len(extra), keep, token, blocks, slots, first_owner)
    anywhere = pl.BlockSpec(memory_space=pl.ANY)
    smem = pl.BlockSpec(memory_space=pltpu.SMEM)
    vmem = pl.BlockSpec(memory_space=pltpu.VMEM)
    mixed = jax.ShapeDtypeStruct((width, here, depth), jnp.bfloat16)
    out = jax.ShapeDtypeStruct((total, groups, SUB, depth), jnp.float32)
    count = len(units)
    return pl.pallas_call(
        functools.partial(panel_kernel, plan=plan),
        in_specs=[smem, vmem]
        + [smem] * len(index)
        + [vmem] * (len(flat) + owners)
        + [anywhere] * len(extra),
        out_specs=[anywhere] + [smem] * token + [vmem] * (count * keep),
        out_shape=[out]
        + [jax.ShapeDtypeStruct((1,), jnp.int32)] * token
        + [mixed] * (count * keep),
        scratch_shapes=[pltpu.VMEM(mixed.shape, mixed.dtype)] * (0 if keep or kept else count)
        + [
            pltpu.VMEM((count, own_groups, here, SUB, depth), jnp.float32),
            pltpu.SemaphoreType.DMA((count, own_groups, len(at[0]))),
        ],
        input_output_aliases={2 + len(index) + len(flat) + owners: 0} if extra else {},
        compiler_params=pltpu.CompilerParams(vmem_limit_bytes=VMEM_LIMIT * MIB),
        cost_estimate=pl.CostEstimate(
            flops=12 * count * here * owners * blocks * rows * slots * depth,
            bytes_accessed=4 * count * here * owners * blocks * rows,
            transcendentals=0,
        ),
        name="panel",
    )(place, green_occ, *index, *flat, *turned, *extra)


def after_kernel(token_ref, array_ref, out_ref):
    out_ref[...] = array_ref[...]


def after(token, array):
    vmem = pl.BlockSpec(memory_space=pltpu.VMEM)
    return pl.pallas_call(
        after_kernel,
        in_specs=[pl.BlockSpec(memory_space=pl.ANY), vmem],
        out_specs=vmem,
        out_shape=jax.ShapeDtypeStruct(array.shape, array.dtype),
        name="after",
    )(token, array)


def cycle(count):
    return list(range(0, count, 2)) + list(range(1, count, 2))[::-1]


def ring(count):
    walk = cycle(count)
    return [
        (2 * walk[n] + e, 2 * walk[(n + 1) % count] + e) for n in range(count) for e in range(2)
    ]


def swap(count):
    return [(n, n ^ 1) for n in range(count)]


def behind(index, steps, count):
    walk = cycle(count)
    return 2 * walk[(walk.index(index // 2) - steps) % count] + index % 2


def on_device(b3c_blocks, pair_index, green_occ, green_virt):
    per_device, slots, depth = b3c_blocks.shape
    blocks = pair_index.shape[0]
    rows = per_device // blocks
    n_row, n_col = lax.axis_size("row"), lax.axis_size("col")
    row, col = lax.axis_index("row"), lax.axis_index("col")
    outer, outer_row = n_col // 2, n_row // 2
    cuts = 2 if blocks % 2 == 0 else 1
    total = n_col * per_device
    groups = n_row * blocks // SUB
    split = 2 * blocks == SUB
    sizes = (blocks, slots, green_occ.shape[0], total, groups, per_device // cuts)
    raw = b3c_blocks.reshape(per_device * slots, depth)

    turn_col = functools.partial(lax.ppermute, axis_name="col", perm=ring(outer))
    swap_col = functools.partial(lax.ppermute, axis_name="col", perm=swap(n_col))
    turn_row = functools.partial(lax.ppermute, axis_name="row", perm=ring(outer_row))
    swap_row = functools.partial(lax.ppermute, axis_name="row", perm=swap(n_row))

    every = [(k, e, n) for k in range(outer) for e in range(2) for n in range(cuts)]
    number = {key: n_row + n for n, key in enumerate(every)}
    table = np.zeros((n_row, n_col, n_row + len(every)), np.int32)
    for r in range(n_row):
        for n in range(n_row):
            table[r, :, n] = behind(r, n // 2, outer_row) ^ (n % 2)
    for c in range(n_col):
        for key in every:
            k, e, cut = key
            table[:, c, number[key]] = (behind(c, k, outer) ^ e) * cuts + cut
    place = lax.dynamic_index_in_dim(
        jnp.asarray(table).reshape(n_row * n_col, -1), row * n_col + col, 0, keepdims=False
    )

    held, kept, state = {}, {}, {"panel": None}
    halves, turned = prepare(raw, pair_index, green_virt, cuts, rows)
    for n, piece in enumerate(halves):
        held[0, 0, n] = piece
    turned = [turned]
    for k in range(outer_row - 1):
        turned.append(turn_row(turned[-1]))
    paired = outer == 4 and cuts == 2 and split and outer_row == 2
    if not paired:
        turned = [a for t in turned for a in (t, swap_row(t))]
    index = [jnp.concatenate([pair_index, swap_row(pair_index)], axis=0)]
    for k in range(outer_row - 1):
        index.append(turn_row(index[-1]))

    def step(k, n):
        held[k, 0, n] = turn_col(held[k - 1, 0, n])

    def cross(k, n):
        held[k, 1, n] = swap_col(held[k, 0, n])

    def panel(units, first, count, keep=False, reuse=False, token=False):
        at = [[number[key] for key in unit] for unit in units]
        data = [[kept[tuple(unit)]] if reuse else [held[key] for key in unit] for unit in units]
        here = index[first // 2 : (first + count) // 2]
        state["panel"], *more = make_panel(
            place, green_occ, here, data, at, turned[first : first + count], first, sizes,
            state["panel"], keep, reuse, token,
        )
        if token:
            return more[0]
        for unit, array in zip(units, more):
            kept[tuple(unit)] = array

    if paired:
        A, B = 0, 1
        turned = [turned[0], swap_row(turned[0]), turned[1]]
        for n in range(2):
            step(1, n)
            cross(0, n)
            step(2, n)
        cross(1, A)
        early = [
            [(0, 0, A), (0, 0, B)], [(1, 0, A), (0, 1, A)], [(1, 0, B), (0, 1, B)]
        ]
        for unit in early[:2]:
            panel([unit], 0, 2, keep=True)
        turned.append(swap_row(turned[2]))
        panel(early[2:], 0, 2, keep=True)
        held[2, 0, A] = after(kept[tuple(early[2])], held[2, 0, A])
        step(3, A)
        cross(2, A)
        token = panel(early, 2, 2, reuse=True, token=True)
        held[2, 0, B] = after(token, held[2, 0, B])
        step(3, B)
        cross(2, B)
        token = panel([[(2, 0, A), (1, 1, A)]], 0, 4, token=True)
        held[3, 0, A] = after(token, held[3, 0, A])
        cross(3, A)
        held[1, 1, B] = turn_col(after(token, held[0, 1, B]))
        token = panel([[(2, 0, B), (2, 1, A)]], 0, 4, token=True)
        held[3, 0, B] = after(token, held[3, 0, B])
        cross(3, B)
        panel([[(3, 0, A), (2, 1, B)]], 0, 4)
        panel([[(3, 0, B), (3, 1, A)]], 0, 4)
        panel([[(1, 1, B), (3, 1, B)]], 0, 4)
    else:
        for k in range(outer):
            for n in range(cuts):
                if k > 0:
                    step(k, n)
                cross(k, n)
        for key in every:
            panel([[key]], 0, n_row)
    return state["panel"].reshape(total, n_row, 1, per_device)


def solution(mesh):
    return jax.shard_map(
        on_device,
        mesh=mesh,
        in_specs=(P(("row", "col"), None, None), P(("row", "col"), None), P(), P()),
        out_specs=P("row", None, "col", None),
        check_vma=False,
    )
```

```python
import functools

import jax
import jax.numpy as jnp
import numpy as np
from jax import lax
from jax.experimental import pallas as pl
from jax.experimental.pallas import tpu as pltpu
from jax.sharding import PartitionSpec as P

GROUP = 32
TAIL = 16
SUB = 8
MIB = 1 << 20
VMEM_LIMIT = 24
EARLY, FULL = 24, 18


def names_of(index_ref, first, count, lanes):
    slots = index_ref.shape[1]
    row = lax.broadcasted_iota(jnp.int32, (TAIL, lanes), 0)
    lane = lax.broadcasted_iota(jnp.int32, (TAIL, lanes), 1) % slots
    names = jnp.zeros((TAIL, lanes), jnp.float32)
    for b in range(count):
        for j in range(slots):
            here = (row == b) & (lane == j)
            names = jnp.where(here, index_ref[first + b, j].astype(jnp.float32), names)
    return names.astype(jnp.bfloat16)


def prepare_kernel(index_ref, raw_ref, virt_ref, *out_refs):
    *half_refs, turned_ref = out_refs
    depth = raw_ref.shape[1]
    blocks, slots = index_ref.shape
    rows = turned_ref.shape[1]
    per_piece = blocks // len(half_refs)
    span = raw_ref.shape[0] // len(half_refs)
    for n, half_ref in enumerate(half_refs):
        half = jnp.dot(
            raw_ref[n * span : (n + 1) * span, :], virt_ref[...], preferred_element_type=jnp.float32
        )
        half_ref[:span, :] = half.astype(jnp.bfloat16)
        half_ref[span:, :] = names_of(index_ref, n * per_piece, per_piece, depth)
    span = GROUP * slots
    to = lax.broadcasted_iota(jnp.int32, (span, span), 0)
    at = lax.broadcasted_iota(jnp.int32, (span, span), 1)
    same = (to // GROUP == at % slots) & (to % GROUP == at // slots)
    move = jnp.where(same, 1.0, 0.0).astype(jnp.bfloat16)
    for b in range(blocks):
        base = b * rows * slots
        parts = [
            jnp.dot(
                move,
                raw_ref[base + g * span : base + (g + 1) * span, :],
                preferred_element_type=jnp.float32,
            )
            for g in range(rows // GROUP)
        ]
        for j in range(slots):
            slab = jnp.concatenate([part[j * GROUP : (j + 1) * GROUP, :] for part in parts], axis=0)
            first = (b * slots + j) * depth
            turned_ref[first : first + depth, :] = slab.T.astype(jnp.bfloat16)


def prepare(raw, pair_index, green_virt, pieces, rows):
    span, depth = raw.shape[0] // pieces, raw.shape[1]
    blocks, slots = pair_index.shape
    vmem = pl.BlockSpec(memory_space=pltpu.VMEM)
    *halves, turned = pl.pallas_call(
        prepare_kernel,
        in_specs=[pl.BlockSpec(memory_space=pltpu.SMEM), vmem, vmem],
        out_specs=[vmem] * (pieces + 1),
        out_shape=[jax.ShapeDtypeStruct((span + TAIL, depth), jnp.bfloat16)] * pieces
        + [jax.ShapeDtypeStruct((blocks * slots * depth, rows), jnp.bfloat16)],
        compiler_params=pltpu.CompilerParams(vmem_limit_bytes=62 * MIB),
        name="prepare",
    )(pair_index, raw, green_virt)
    return halves, turned


def mix_pieces(occ_ref, piece_refs, mixed_ref, rows, slots):
    width, _, depth = mixed_ref.shape
    span = piece_refs[0].shape[0] - TAIL
    per_piece = span // (rows * slots)
    wide = GROUP * slots
    level = lax.broadcasted_iota(jnp.int32, (width, wide), 0).astype(jnp.float32)
    to = lax.broadcasted_iota(jnp.int32, (width * GROUP, wide), 0) % GROUP
    at = lax.broadcasted_iota(jnp.int32, (width * GROUP, wide), 1) // slots
    same = to == at
    for n, piece_ref in enumerate(piece_refs):
        names = piece_ref[span:, :].astype(jnp.float32)
        for b in range(per_piece):
            name = jnp.concatenate([names[b : b + 1, :]] * (wide // depth), axis=1)
            named = jnp.where(level == name, 1.0, 0.0).astype(jnp.bfloat16)
            picked = lax.dot_general(
                occ_ref[...], named, (((0,), (0,)), ((), ())), preferred_element_type=jnp.float32
            )
            mix = jnp.broadcast_to(picked[:, None, :], (width, GROUP, wide))
            mix = jnp.where(same, mix.reshape(width * GROUP, wide), 0.0).astype(jnp.bfloat16)
            base = b * rows * slots
            for g in range(0, rows // GROUP, 2):
                right = jnp.concatenate(
                    [
                        piece_ref[base + (g + e) * wide : base + (g + e + 1) * wide, :]
                        for e in range(2)
                    ],
                    axis=1,
                )
                part = jnp.dot(mix, right, preferred_element_type=jnp.float32).astype(jnp.bfloat16)
                for e in range(2):
                    first = (n * per_piece + b) * rows + (g + e) * GROUP
                    mixed_ref[:, first : first + GROUP, :] = part[
                        :, e * depth : (e + 1) * depth
                    ].reshape(width, GROUP, depth)


def panel_kernel(place_ref, occ_ref, *rest, plan):
    (units, kept, owners, extra, keep, token, blocks, slots, first_owner) = plan
    rest = list(rest)
    take = lambda count: [rest.pop(0) for _ in range(count)]
    index_refs = take(owners // 2)
    unit_refs = [take(1 if kept else len(unit)) for unit in units]
    turned_refs = take(owners)
    take(extra)
    out_ref = rest.pop(0)
    for token_ref in take(token):
        token_ref[0] = 0
    mixed_refs = [refs[0] for refs in unit_refs] if kept else take(len(units))
    out_buf, out_sem = rest
    here, depth = mixed_refs[0].shape[1:]
    height = here // len(units[0])
    per_group = SUB // blocks
    stores = []
    here_too = place_ref[0] >= 0
    for u, unit in enumerate(units):
        mixed_ref = mixed_refs[u]
        if not kept:

            @pl.when(here_too)
            def _():
                rows = turned_refs[0].shape[1]
                mix_pieces(occ_ref, unit_refs[u], mixed_ref, rows, slots)

        for g in range(owners // per_group):
            flat = out_buf.at[u, g].reshape(here * SUB, depth)
            tile = place_ref[first_owner + g * per_group] * blocks

            @pl.when(here_too)
            def _():
                for n in range(g * per_group, (g + 1) * per_group):
                    first = lax.rem(place_ref[first_owner + n] * blocks, SUB)
                    for b in range(blocks):
                        left = jnp.concatenate(
                            [
                                mixed_ref[index_refs[n // 2][n % 2 * blocks + b, j]]
                                for j in range(slots)
                            ],
                            axis=1,
                        )
                        right = turned_refs[n][b * slots * depth : (b + 1) * slots * depth, :]
                        flat[pl.ds(first + b, here, stride=SUB), :] = jnp.dot(
                            left, right, preferred_element_type=jnp.float32
                        )

            for n, at in enumerate(unit):
                first = pl.multiple_of(place_ref[at] * height, height)
                store = pltpu.make_async_copy(
                    out_buf.at[u, g, pl.ds(n * height, height)],
                    out_ref.at[pl.ds(first, height), tile // SUB],
                    out_sem.at[u, g, n],
                )
                store.start()
                stores.append(store)
    for store in stores:
        store.wait()


def make_panel(
    place, green_occ, index, units, at, turned, first_owner, sizes, before, keep, kept, token
):
    blocks, slots, width, total, groups, height = sizes
    depth, rows = turned[0].shape[0] // (blocks * slots), turned[0].shape[1]
    owners = len(turned)
    here = len(at[0]) * height
    own_groups = owners * blocks // SUB
    extra = [] if before is None else [before]
    flat = [a for unit in units for a in unit]
    plan = (at, kept, owners, len(extra), keep, token, blocks, slots, first_owner)
    anywhere = pl.BlockSpec(memory_space=pl.ANY)
    smem = pl.BlockSpec(memory_space=pltpu.SMEM)
    vmem = pl.BlockSpec(memory_space=pltpu.VMEM)
    mixed = jax.ShapeDtypeStruct((width, here, depth), jnp.bfloat16)
    out = jax.ShapeDtypeStruct((total, groups, SUB, depth), jnp.float32)
    count = len(units)
    return pl.pallas_call(
        functools.partial(panel_kernel, plan=plan),
        in_specs=[smem, vmem]
        + [smem] * len(index)
        + [vmem] * (len(flat) + owners)
        + [anywhere] * len(extra),
        out_specs=[anywhere] + [smem] * token + [vmem] * (count * keep),
        out_shape=[out]
        + [jax.ShapeDtypeStruct((1,), jnp.int32)] * token
        + [mixed] * (count * keep),
        scratch_shapes=[pltpu.VMEM(mixed.shape, mixed.dtype)] * (0 if keep or kept else count)
        + [
            pltpu.VMEM((count, own_groups, here, SUB, depth), jnp.float32),
            pltpu.SemaphoreType.DMA((count, own_groups, len(at[0]))),
        ],
        input_output_aliases={2 + len(index) + len(flat) + owners: 0} if extra else {},
        compiler_params=pltpu.CompilerParams(vmem_limit_bytes=VMEM_LIMIT * MIB),
        cost_estimate=pl.CostEstimate(
            flops=(EARLY if keep else FULL) * count * here * owners * blocks * rows * slots * depth,
            bytes_accessed=4 * count * here * owners * blocks * rows,
            transcendentals=0,
        ),
        name="panel",
    )(place, green_occ, *index, *flat, *turned, *extra)


def after_kernel(token_ref, array_ref, out_ref):
    out_ref[...] = array_ref[...]


def after(token, array):
    vmem = pl.BlockSpec(memory_space=pltpu.VMEM)
    return pl.pallas_call(
        after_kernel,
        in_specs=[pl.BlockSpec(memory_space=pl.ANY), vmem],
        out_specs=vmem,
        out_shape=jax.ShapeDtypeStruct(array.shape, array.dtype),
        compiler_params=pltpu.CompilerParams(vmem_limit_bytes=4 * MIB),
        name="after",
    )(token, array)


def cycle(count):
    return list(range(0, count, 2)) + list(range(1, count, 2))[::-1]


def ring(count):
    walk = cycle(count)
    return [
        (2 * walk[n] + e, 2 * walk[(n + 1) % count] + e) for n in range(count) for e in range(2)
    ]


def swap(count):
    return [(n, n ^ 1) for n in range(count)]


def behind(index, steps, count):
    walk = cycle(count)
    return 2 * walk[(walk.index(index // 2) - steps) % count] + index % 2


def on_device(b3c_blocks, pair_index, green_occ, green_virt):
    per_device, slots, depth = b3c_blocks.shape
    blocks = pair_index.shape[0]
    rows = per_device // blocks
    n_row, n_col = lax.axis_size("row"), lax.axis_size("col")
    row, col = lax.axis_index("row"), lax.axis_index("col")
    outer, outer_row = n_col // 2, n_row // 2
    cuts = 2 if blocks % 2 == 0 else 1
    total = n_col * per_device
    groups = n_row * blocks // SUB
    split = 2 * blocks == SUB
    sizes = (blocks, slots, green_occ.shape[0], total, groups, per_device // cuts)
    raw = b3c_blocks.reshape(per_device * slots, depth)

    turn_col = functools.partial(lax.ppermute, axis_name="col", perm=ring(outer))
    swap_col = functools.partial(lax.ppermute, axis_name="col", perm=swap(n_col))
    turn_row = functools.partial(lax.ppermute, axis_name="row", perm=ring(outer_row))
    swap_row = functools.partial(lax.ppermute, axis_name="row", perm=swap(n_row))

    every = [(k, e, n) for k in range(outer) for e in range(2) for n in range(cuts)]
    number = {key: n_row + n for n, key in enumerate(every)}
    table = np.zeros((n_row, n_col, n_row + len(every)), np.int32)
    for r in range(n_row):
        for n in range(n_row):
            table[r, :, n] = behind(r, n // 2, outer_row) ^ (n % 2)
    for c in range(n_col):
        for key in every:
            k, e, cut = key
            table[:, c, number[key]] = (behind(c, k, outer) ^ e) * cuts + cut
    place = lax.dynamic_index_in_dim(
        jnp.asarray(table).reshape(n_row * n_col, -1), row * n_col + col, 0, keepdims=False
    )

    held, kept, state = {}, {}, {"panel": None}
    halves, turned = prepare(raw, pair_index, green_virt, cuts, rows)
    for n, piece in enumerate(halves):
        held[0, 0, n] = piece
    turned = [turned]
    for k in range(outer_row - 1):
        turned.append(turn_row(turned[-1]))
    paired = outer == 4 and cuts == 2 and split and outer_row == 2
    if not paired:
        turned = [a for t in turned for a in (t, swap_row(t))]
    index = [jnp.concatenate([pair_index, swap_row(pair_index)], axis=0)]
    for k in range(outer_row - 1):
        index.append(turn_row(index[-1]))

    def step(k, n):
        held[k, 0, n] = turn_col(held[k - 1, 0, n])

    def cross(k, n):
        held[k, 1, n] = swap_col(held[k, 0, n])

    def panel(units, first, count, keep=False, reuse=False, token=False):
        at = [[number[key] for key in unit] for unit in units]
        data = [[kept[tuple(unit)]] if reuse else [held[key] for key in unit] for unit in units]
        here = index[first // 2 : (first + count) // 2]
        state["panel"], *more = make_panel(
            place, green_occ, here, data, at, turned[first : first + count], first, sizes,
            state["panel"], keep, reuse, token,
        )
        if token:
            return more[0]
        for unit, array in zip(units, more):
            kept[tuple(unit)] = array

    if paired:
        A, B = 0, 1
        turned = [turned[0], swap_row(turned[0]), turned[1]]
        for n in range(2):
            step(1, n)
            cross(0, n)
            step(2, n)
        cross(1, A)
        early = [
            [(0, 0, A), (0, 0, B)], [(1, 0, A), (0, 1, A)], [(1, 0, B), (0, 1, B)]
        ]
        for unit in early[:2]:
            panel([unit], 0, 2, keep=True)
        turned.append(swap_row(turned[2]))
        panel(early[2:], 0, 2, keep=True)
        held[2, 0, A] = after(kept[tuple(early[2])], held[2, 0, A])
        step(3, A)
        cross(2, A)
        token = panel(early, 2, 2, reuse=True, token=True)
        held[2, 0, B] = after(token, held[2, 0, B])
        step(3, B)
        cross(2, B)
        token = panel([[(2, 0, A), (1, 1, A)]], 0, 4, token=True)
        held[3, 0, A] = after(token, held[3, 0, A])
        cross(3, A)
        held[1, 1, B] = turn_col(after(token, held[0, 1, B]))
        token = panel([[(2, 0, B), (2, 1, A)]], 0, 4, token=True)
        held[3, 0, B] = after(token, held[3, 0, B])
        cross(3, B)
        panel([[(3, 0, A), (2, 1, B)], [(3, 0, B), (3, 1, A)]], 0, 4)
        panel([[(1, 1, B), (3, 1, B)]], 0, 4)
    else:
        for k in range(outer):
            for n in range(cuts):
                if k > 0:
                    step(k, n)
                cross(k, n)
        for key in every:
            panel([[key]], 0, n_row)
    return state["panel"].reshape(total, n_row, 1, per_device)


def solution(mesh):
    return jax.shard_map(
        on_device,
        mesh=mesh,
        in_specs=(P(("row", "col"), None, None), P(("row", "col"), None), P(), P()),
        out_specs=P("row", None, "col", None),
        check_vma=False,
    )
```

```python
import functools

import jax
import jax.numpy as jnp
import numpy as np
from jax import lax
from jax.experimental import pallas as pl
from jax.experimental.pallas import tpu as pltpu
from jax.sharding import PartitionSpec as P

GROUP = 32
TAIL = 16
SUB = 8
MIB = 1 << 20
VMEM_LIMIT = 24
PREPARE = 62
EARLY, FULL = 24, 18


def names_of(index_ref, first, count, lanes):
    slots = index_ref.shape[1]
    row = lax.broadcasted_iota(jnp.int32, (TAIL, lanes), 0)
    lane = lax.broadcasted_iota(jnp.int32, (TAIL, lanes), 1) % slots
    names = jnp.zeros((TAIL, lanes), jnp.float32)
    for b in range(count):
        for j in range(slots):
            here = (row == b) & (lane == j)
            names = jnp.where(here, index_ref[first + b, j].astype(jnp.float32), names)
    return names.astype(jnp.bfloat16)


def prepare_kernel(table_ref, index_ref, raw_ref, virt_ref, occ_ref, *out_refs):
    *half_refs, turned_ref, turned_occ_ref, place_ref = out_refs
    device = lax.axis_index("row") * lax.axis_size("col") + lax.axis_index("col")
    for n in range(place_ref.shape[0]):
        place_ref[n] = table_ref[device, n]
    turned_occ_ref[...] = occ_ref[...].astype(jnp.float32).T.astype(jnp.bfloat16)
    depth = raw_ref.shape[1]
    blocks, slots = index_ref.shape
    rows = turned_ref.shape[1]
    per_piece = blocks // len(half_refs)
    span = raw_ref.shape[0] // len(half_refs)
    for n, half_ref in enumerate(half_refs):
        half = jnp.dot(
            raw_ref[n * span : (n + 1) * span, :], virt_ref[...], preferred_element_type=jnp.float32
        )
        half_ref[:span, :] = half.astype(jnp.bfloat16)
        half_ref[span:, :] = names_of(index_ref, n * per_piece, per_piece, depth)
    span = GROUP * slots
    to = lax.broadcasted_iota(jnp.int32, (span, span), 0)
    at = lax.broadcasted_iota(jnp.int32, (span, span), 1)
    same = (to // GROUP == at % slots) & (to % GROUP == at // slots)
    move = jnp.where(same, 1.0, 0.0).astype(jnp.bfloat16)
    for b in range(blocks):
        base = b * rows * slots
        parts = [
            jnp.dot(
                move,
                raw_ref[base + g * span : base + (g + 1) * span, :],
                preferred_element_type=jnp.float32,
            )
            for g in range(rows // GROUP)
        ]
        for j in range(slots):
            slab = jnp.concatenate([part[j * GROUP : (j + 1) * GROUP, :] for part in parts], axis=0)
            first = (b * slots + j) * depth
            turned_ref[first : first + depth, :] = slab.T.astype(jnp.bfloat16)


def prepare(table, raw, pair_index, green_virt, green_occ, pieces, rows):
    span, depth = raw.shape[0] // pieces, raw.shape[1]
    blocks, slots = pair_index.shape
    vmem = pl.BlockSpec(memory_space=pltpu.VMEM)
    smem = pl.BlockSpec(memory_space=pltpu.SMEM)
    *halves, turned, turned_occ, place = pl.pallas_call(
        prepare_kernel,
        in_specs=[smem, smem, vmem, vmem, vmem],
        out_specs=[vmem] * (pieces + 2) + [smem],
        out_shape=[jax.ShapeDtypeStruct((span + TAIL, depth), jnp.bfloat16)] * pieces
        + [
            jax.ShapeDtypeStruct((blocks * slots * depth, rows), jnp.bfloat16),
            jax.ShapeDtypeStruct(green_occ.shape, jnp.bfloat16),
            jax.ShapeDtypeStruct(table.shape[1:], jnp.int32),
        ],
        compiler_params=pltpu.CompilerParams(vmem_limit_bytes=PREPARE * MIB),
        name="prepare",
    )(table, pair_index, raw, green_virt, green_occ)
    return halves, turned, turned_occ, place


def mix_pieces(occ_ref, piece_refs, mixed_ref, rows, slots):
    width, _, depth = mixed_ref.shape
    span = piece_refs[0].shape[0] - TAIL
    per_piece = span // (rows * slots)
    wide = GROUP * slots
    level = lax.broadcasted_iota(jnp.int32, (width, wide), 0).astype(jnp.float32)
    to = lax.broadcasted_iota(jnp.int32, (width * GROUP, wide), 0) % GROUP
    same = to == lax.broadcasted_iota(jnp.int32, (width * GROUP, wide), 1) // slots
    named = []
    for piece_ref in piece_refs:
        names = piece_ref[span:, :].astype(jnp.float32)
        for b in range(per_piece):
            name = jnp.concatenate([names[b : b + 1, :]] * (wide // depth), axis=1)
            named.append(jnp.where(level == name, 1.0, 0.0).astype(jnp.bfloat16))
    picked = jnp.dot(
        occ_ref[...], jnp.concatenate(named, axis=1), preferred_element_type=jnp.float32
    )
    for n, piece_ref in enumerate(piece_refs):
        for b in range(per_piece):
            at = (n * per_piece + b) * wide
            mix = jnp.broadcast_to(picked[:, None, at : at + wide], (width, GROUP, wide))
            mix = jnp.where(same, mix.reshape(width * GROUP, wide), 0.0).astype(jnp.bfloat16)
            base = b * rows * slots
            for g in range(0, rows // GROUP, 2):
                right = jnp.concatenate(
                    [
                        piece_ref[base + (g + e) * wide : base + (g + e + 1) * wide, :]
                        for e in range(2)
                    ],
                    axis=1,
                )
                part = jnp.dot(mix, right, preferred_element_type=jnp.float32).astype(jnp.bfloat16)
                for e in range(2):
                    first = (n * per_piece + b) * rows + (g + e) * GROUP
                    mixed_ref[:, first : first + GROUP, :] = part[
                        :, e * depth : (e + 1) * depth
                    ].reshape(width, GROUP, depth)


def panel_kernel(place_ref, occ_ref, *rest, plan):
    (units, kept, owners, extra, keep, token, blocks, slots, first_owner) = plan
    rest = list(rest)
    take = lambda count: [rest.pop(0) for _ in range(count)]
    index_refs = take(owners // 2)
    unit_refs = [take(1 if kept else len(unit)) for unit in units]
    turned_refs = take(owners)
    take(extra)
    out_ref = rest.pop(0)
    for token_ref in take(token):
        token_ref[0] = 0
    mixed_refs = [refs[0] for refs in unit_refs] if kept else take(len(units))
    out_buf, out_sem = rest
    here, depth = mixed_refs[0].shape[1:]
    height = here // len(units[0])
    per_group = SUB // blocks
    stores = []
    here_too = place_ref[0] >= 0
    for u, unit in enumerate(units):
        mixed_ref = mixed_refs[u]
        if not kept:

            @pl.when(here_too)
            def _():
                rows = turned_refs[0].shape[1]
                mix_pieces(occ_ref, unit_refs[u], mixed_ref, rows, slots)

        for g in range(owners // per_group):
            flat = out_buf.at[u, g].reshape(here * SUB, depth)
            tile = place_ref[first_owner + g * per_group] * blocks

            @pl.when(here_too)
            def _():
                for n in range(g * per_group, (g + 1) * per_group):
                    first = lax.rem(place_ref[first_owner + n] * blocks, SUB)
                    for b in range(blocks):
                        left = jnp.concatenate(
                            [
                                mixed_ref[index_refs[n // 2][n % 2 * blocks + b, j]]
                                for j in range(slots)
                            ],
                            axis=1,
                        )
                        right = turned_refs[n][b * slots * depth : (b + 1) * slots * depth, :]
                        flat[pl.ds(first + b, here, stride=SUB), :] = jnp.dot(
                            left, right, preferred_element_type=jnp.float32
                        )

            for n, at in enumerate(unit):
                first = pl.multiple_of(place_ref[at] * height, height)
                store = pltpu.make_async_copy(
                    out_buf.at[u, g, pl.ds(n * height, height)],
                    out_ref.at[pl.ds(first, height), tile // SUB],
                    out_sem.at[u, g, n],
                )
                store.start()
                stores.append(store)
    for store in stores:
        store.wait()


def make_panel(
    place, green_occ, index, units, at, turned, first_owner, sizes, before, keep, kept, token
):
    blocks, slots, width, total, groups, height = sizes
    depth, rows = turned[0].shape[0] // (blocks * slots), turned[0].shape[1]
    owners = len(turned)
    here = len(at[0]) * height
    own_groups = owners * blocks // SUB
    extra = [] if before is None else [before]
    flat = [a for unit in units for a in unit]
    plan = (at, kept, owners, len(extra), keep, token, blocks, slots, first_owner)
    anywhere = pl.BlockSpec(memory_space=pl.ANY)
    smem = pl.BlockSpec(memory_space=pltpu.SMEM)
    vmem = pl.BlockSpec(memory_space=pltpu.VMEM)
    mixed = jax.ShapeDtypeStruct((width, here, depth), jnp.bfloat16)
    out = jax.ShapeDtypeStruct((total, groups, SUB, depth), jnp.float32)
    count = len(units)
    return pl.pallas_call(
        functools.partial(panel_kernel, plan=plan),
        in_specs=[smem, vmem]
        + [smem] * len(index)
        + [vmem] * (len(flat) + owners)
        + [anywhere] * len(extra),
        out_specs=[anywhere] + [smem] * token + [vmem] * (count * keep),
        out_shape=[out]
        + [jax.ShapeDtypeStruct((1,), jnp.int32)] * token
        + [mixed] * (count * keep),
        scratch_shapes=[pltpu.VMEM(mixed.shape, mixed.dtype)] * (0 if keep or kept else count)
        + [
            pltpu.VMEM((count, own_groups, here, SUB, depth), jnp.float32),
            pltpu.SemaphoreType.DMA((count, own_groups, len(at[0]))),
        ],
        input_output_aliases={2 + len(index) + len(flat) + owners: 0} if extra else {},
        compiler_params=pltpu.CompilerParams(vmem_limit_bytes=VMEM_LIMIT * MIB),
        cost_estimate=pl.CostEstimate(
            flops=(EARLY if keep else FULL) * count * here * owners * blocks * rows * slots * depth,
            bytes_accessed=4 * count * here * owners * blocks * rows,
            transcendentals=0,
        ),
        name="panel",
    )(place, green_occ, *index, *flat, *turned, *extra)


def after_kernel(token_ref, array_ref, out_ref):
    out_ref[...] = array_ref[...]


def after(token, array):
    vmem = pl.BlockSpec(memory_space=pltpu.VMEM)
    return pl.pallas_call(
        after_kernel,
        in_specs=[pl.BlockSpec(memory_space=pl.ANY), vmem],
        out_specs=vmem,
        out_shape=jax.ShapeDtypeStruct(array.shape, array.dtype),
        compiler_params=pltpu.CompilerParams(vmem_limit_bytes=4 * MIB),
        name="after",
    )(token, array)


def cycle(count):
    return list(range(0, count, 2)) + list(range(1, count, 2))[::-1]


def ring(count):
    walk = cycle(count)
    return [
        (2 * walk[n] + e, 2 * walk[(n + 1) % count] + e) for n in range(count) for e in range(2)
    ]


def swap(count):
    return [(n, n ^ 1) for n in range(count)]


def behind(index, steps, count):
    walk = cycle(count)
    return 2 * walk[(walk.index(index // 2) - steps) % count] + index % 2


def on_device(b3c_blocks, pair_index, green_occ, green_virt):
    per_device, slots, depth = b3c_blocks.shape
    blocks = pair_index.shape[0]
    rows = per_device // blocks
    n_row, n_col = lax.axis_size("row"), lax.axis_size("col")
    outer, outer_row = n_col // 2, n_row // 2
    cuts = 2 if blocks % 2 == 0 else 1
    total = n_col * per_device
    groups = n_row * blocks // SUB
    split = 2 * blocks == SUB
    sizes = (blocks, slots, green_occ.shape[0], total, groups, per_device // cuts)
    raw = b3c_blocks.reshape(per_device * slots, depth)

    turn_col = functools.partial(lax.ppermute, axis_name="col", perm=ring(outer))
    swap_col = functools.partial(lax.ppermute, axis_name="col", perm=swap(n_col))
    turn_row = functools.partial(lax.ppermute, axis_name="row", perm=ring(outer_row))
    swap_row = functools.partial(lax.ppermute, axis_name="row", perm=swap(n_row))

    every = [(k, e, n) for k in range(outer) for e in range(2) for n in range(cuts)]
    number = {key: n_row + n for n, key in enumerate(every)}
    table = np.zeros((n_row, n_col, n_row + len(every)), np.int32)
    for r in range(n_row):
        for n in range(n_row):
            table[r, :, n] = behind(r, n // 2, outer_row) ^ (n % 2)
    for c in range(n_col):
        for key in every:
            k, e, cut = key
            table[:, c, number[key]] = (behind(c, k, outer) ^ e) * cuts + cut
    held, kept, state = {}, {}, {"panel": None}
    halves, turned, turned_occ, place = prepare(
        jnp.asarray(table).reshape(n_row * n_col, -1), raw, pair_index, green_virt, green_occ,
        cuts, rows,
    )
    for n, piece in enumerate(halves):
        held[0, 0, n] = piece
    turned = [turned]
    for k in range(outer_row - 1):
        turned.append(turn_row(turned[-1]))
    paired = outer == 4 and cuts == 2 and split and outer_row == 2
    if not paired:
        turned = [a for t in turned for a in (t, swap_row(t))]
    index = [jnp.concatenate([pair_index, swap_row(pair_index)], axis=0)]
    for k in range(outer_row - 1):
        index.append(turn_row(index[-1]))

    def step(k, n):
        held[k, 0, n] = turn_col(held[k - 1, 0, n])

    def cross(k, n):
        held[k, 1, n] = swap_col(held[k, 0, n])

    def panel(units, first, count, keep=False, reuse=False, token=False):
        at = [[number[key] for key in unit] for unit in units]
        data = [[kept[tuple(unit)]] if reuse else [held[key] for key in unit] for unit in units]
        here = index[first // 2 : (first + count) // 2]
        state["panel"], *more = make_panel(
            place, turned_occ, here, data, at, turned[first : first + count], first, sizes,
            state["panel"], keep, reuse, token,
        )
        if token:
            return more[0]
        for unit, array in zip(units, more):
            kept[tuple(unit)] = array

    if paired:
        A, B = 0, 1
        turned = [turned[0], swap_row(turned[0]), turned[1]]
        for n in range(2):
            step(1, n)
            cross(0, n)
            step(2, n)
        cross(1, A)
        early = [
            [(0, 0, A), (0, 0, B)], [(1, 0, A), (0, 1, A)], [(1, 0, B), (0, 1, B)]
        ]
        for unit in early[:2]:
            panel([unit], 0, 2, keep=True)
        turned.append(swap_row(turned[2]))
        panel(early[2:], 0, 2, keep=True)
        held[2, 0, A] = after(kept[tuple(early[2])], held[2, 0, A])
        step(3, A)
        cross(2, A)
        token = panel(early, 2, 2, reuse=True, token=True)
        held[2, 0, B] = after(token, held[2, 0, B])
        step(3, B)
        cross(2, B)
        token = panel([[(2, 0, A), (1, 1, A)]], 0, 4, token=True)
        held[3, 0, A] = after(token, held[3, 0, A])
        cross(3, A)
        held[1, 1, B] = turn_col(after(token, held[0, 1, B]))
        token = panel([[(2, 0, B), (2, 1, A)]], 0, 4, token=True)
        held[3, 0, B] = after(token, held[3, 0, B])
        cross(3, B)
        panel([[(3, 0, A), (2, 1, B)], [(3, 0, B), (3, 1, A)]], 0, 4)
        panel([[(1, 1, B), (3, 1, B)]], 0, 4)
    else:
        for k in range(outer):
            for n in range(cuts):
                if k > 0:
                    step(k, n)
                cross(k, n)
        for key in every:
            panel([[key]], 0, n_row)
    return state["panel"].reshape(total, n_row, 1, per_device)


def solution(mesh):
    return jax.shard_map(
        on_device,
        mesh=mesh,
        in_specs=(P(("row", "col"), None, None), P(("row", "col"), None), P(), P()),
        out_specs=P("row", None, "col", None),
        check_vma=False,
    )
```

```python
import functools

import jax
import jax.numpy as jnp
import numpy as np
from jax import lax
from jax.experimental import pallas as pl
from jax.experimental.pallas import tpu as pltpu
from jax.sharding import PartitionSpec as P

GROUP = 32
TAIL = 16
SUB = 8
MIB = 1 << 20
VMEM_LIMIT = 24
EARLY, FULL = 24, 18


def names_of(index_ref, first, count, lanes):
    slots = index_ref.shape[1]
    row = lax.broadcasted_iota(jnp.int32, (TAIL, lanes), 0)
    lane = lax.broadcasted_iota(jnp.int32, (TAIL, lanes), 1) % slots
    names = jnp.zeros((TAIL, lanes), jnp.float32)
    for b in range(count):
        for j in range(slots):
            here = (row == b) & (lane == j)
            names = jnp.where(here, index_ref[first + b, j].astype(jnp.float32), names)
    return names.astype(jnp.bfloat16)


def prepare_kernel(index_ref, raw_ref, virt_ref, *out_refs):
    *half_refs, turned_ref = out_refs
    depth = raw_ref.shape[1]
    blocks, slots = index_ref.shape
    rows = turned_ref.shape[1]
    per_piece = blocks // len(half_refs)
    span = raw_ref.shape[0] // len(half_refs)
    for n, half_ref in enumerate(half_refs):
        half = jnp.dot(
            raw_ref[n * span : (n + 1) * span, :], virt_ref[...], preferred_element_type=jnp.float32
        )
        half_ref[:span, :] = half.astype(jnp.bfloat16)
        half_ref[span:, :] = names_of(index_ref, n * per_piece, per_piece, depth)
    span = GROUP * slots
    to = lax.broadcasted_iota(jnp.int32, (span, span), 0)
    at = lax.broadcasted_iota(jnp.int32, (span, span), 1)
    same = (to // GROUP == at % slots) & (to % GROUP == at // slots)
    move = jnp.where(same, 1.0, 0.0).astype(jnp.bfloat16)
    for b in range(blocks):
        base = b * rows * slots
        parts = [
            jnp.dot(
                move,
                raw_ref[base + g * span : base + (g + 1) * span, :],
                preferred_element_type=jnp.float32,
            )
            for g in range(rows // GROUP)
        ]
        for j in range(slots):
            slab = jnp.concatenate([part[j * GROUP : (j + 1) * GROUP, :] for part in parts], axis=0)
            first = (b * slots + j) * depth
            turned_ref[first : first + depth, :] = slab.T.astype(jnp.bfloat16)


def prepare(raw, pair_index, green_virt, pieces, rows):
    span, depth = raw.shape[0] // pieces, raw.shape[1]
    blocks, slots = pair_index.shape
    vmem = pl.BlockSpec(memory_space=pltpu.VMEM)
    *halves, turned = pl.pallas_call(
        prepare_kernel,
        in_specs=[pl.BlockSpec(memory_space=pltpu.SMEM), vmem, vmem],
        out_specs=[vmem] * (pieces + 1),
        out_shape=[jax.ShapeDtypeStruct((span + TAIL, depth), jnp.bfloat16)] * pieces
        + [jax.ShapeDtypeStruct((blocks * slots * depth, rows), jnp.bfloat16)],
        compiler_params=pltpu.CompilerParams(vmem_limit_bytes=62 * MIB),
        name="prepare",
    )(pair_index, raw, green_virt)
    return halves, turned


def mix_pieces(occ_ref, piece_refs, mixed_ref, rows, slots):
    width, _, depth = mixed_ref.shape
    span = piece_refs[0].shape[0] - TAIL
    per_piece = span // (rows * slots)
    wide = GROUP * slots
    level = lax.broadcasted_iota(jnp.int32, (width, wide), 0).astype(jnp.float32)
    to = lax.broadcasted_iota(jnp.int32, (width * GROUP, wide), 0) % GROUP
    same = to == lax.broadcasted_iota(jnp.int32, (width * GROUP, wide), 1) // slots
    named = []
    for piece_ref in piece_refs:
        names = piece_ref[span:, :].astype(jnp.float32)
        for b in range(per_piece):
            name = jnp.concatenate([names[b : b + 1, :]] * (wide // depth), axis=1)
            named.append(jnp.where(level == name, 1.0, 0.0).astype(jnp.bfloat16))
    picked = lax.dot_general(
        occ_ref[...],
        jnp.concatenate(named, axis=1),
        (((0,), (0,)), ((), ())),
        preferred_element_type=jnp.float32,
    )
    for n, piece_ref in enumerate(piece_refs):
        for b in range(per_piece):
            at = (n * per_piece + b) * wide
            mix = jnp.broadcast_to(picked[:, None, at : at + wide], (width, GROUP, wide))
            mix = jnp.where(same, mix.reshape(width * GROUP, wide), 0.0).astype(jnp.bfloat16)
            base = b * rows * slots
            for g in range(0, rows // GROUP, 2):
                right = jnp.concatenate(
                    [
                        piece_ref[base + (g + e) * wide : base + (g + e + 1) * wide, :]
                        for e in range(2)
                    ],
                    axis=1,
                )
                part = jnp.dot(mix, right, preferred_element_type=jnp.float32).astype(jnp.bfloat16)
                for e in range(2):
                    first = (n * per_piece + b) * rows + (g + e) * GROUP
                    mixed_ref[:, first : first + GROUP, :] = part[
                        :, e * depth : (e + 1) * depth
                    ].reshape(width, GROUP, depth)


def panel_kernel(place_ref, occ_ref, *rest, plan):
    (units, kept, owners, extra, keep, token, blocks, slots, first_owner) = plan
    rest = list(rest)
    take = lambda count: [rest.pop(0) for _ in range(count)]
    index_refs = take(owners // 2)
    unit_refs = [take(1 if kept else len(unit)) for unit in units]
    turned_refs = take(owners)
    take(extra)
    out_ref = rest.pop(0)
    for token_ref in take(token):
        token_ref[0] = 0
    mixed_refs = [refs[0] for refs in unit_refs] if kept else take(len(units))
    out_buf, out_sem = rest
    here, depth = mixed_refs[0].shape[1:]
    height = here // len(units[0])
    per_group = SUB // blocks
    stores = []
    here_too = place_ref[0] >= 0
    for u, unit in enumerate(units):
        mixed_ref = mixed_refs[u]
        if not kept:

            @pl.when(here_too)
            def _():
                rows = turned_refs[0].shape[1]
                mix_pieces(occ_ref, unit_refs[u], mixed_ref, rows, slots)

        for g in range(owners // per_group):
            flat = out_buf.at[u, g].reshape(here * SUB, depth)
            tile = place_ref[first_owner + g * per_group] * blocks

            @pl.when(here_too)
            def _():
                for n in range(g * per_group, (g + 1) * per_group):
                    first = lax.rem(place_ref[first_owner + n] * blocks, SUB)
                    for b in range(blocks):
                        left = jnp.concatenate(
                            [
                                mixed_ref[index_refs[n // 2][n % 2 * blocks + b, j]]
                                for j in range(slots)
                            ],
                            axis=1,
                        )
                        right = turned_refs[n][b * slots * depth : (b + 1) * slots * depth, :]
                        flat[pl.ds(first + b, here, stride=SUB), :] = jnp.dot(
                            left, right, preferred_element_type=jnp.float32
                        )

            for n, at in enumerate(unit):
                first = pl.multiple_of(place_ref[at] * height, height)
                store = pltpu.make_async_copy(
                    out_buf.at[u, g, pl.ds(n * height, height)],
                    out_ref.at[pl.ds(first, height), tile // SUB],
                    out_sem.at[u, g, n],
                )
                store.start()
                stores.append(store)
    for store in stores:
        store.wait()


def make_panel(
    place, green_occ, index, units, at, turned, first_owner, sizes, before, keep, kept, token
):
    blocks, slots, width, total, groups, height = sizes
    depth, rows = turned[0].shape[0] // (blocks * slots), turned[0].shape[1]
    owners = len(turned)
    here = len(at[0]) * height
    own_groups = owners * blocks // SUB
    extra = [] if before is None else [before]
    flat = [a for unit in units for a in unit]
    plan = (at, kept, owners, len(extra), keep, token, blocks, slots, first_owner)
    anywhere = pl.BlockSpec(memory_space=pl.ANY)
    smem = pl.BlockSpec(memory_space=pltpu.SMEM)
    vmem = pl.BlockSpec(memory_space=pltpu.VMEM)
    mixed = jax.ShapeDtypeStruct((width, here, depth), jnp.bfloat16)
    out = jax.ShapeDtypeStruct((total, groups, SUB, depth), jnp.float32)
    count = len(units)
    return pl.pallas_call(
        functools.partial(panel_kernel, plan=plan),
        in_specs=[smem, vmem]
        + [smem] * len(index)
        + [vmem] * (len(flat) + owners)
        + [anywhere] * len(extra),
        out_specs=[anywhere] + [smem] * token + [vmem] * (count * keep),
        out_shape=[out]
        + [jax.ShapeDtypeStruct((1,), jnp.int32)] * token
        + [mixed] * (count * keep),
        scratch_shapes=[pltpu.VMEM(mixed.shape, mixed.dtype)] * (0 if keep or kept else count)
        + [
            pltpu.VMEM((count, own_groups, here, SUB, depth), jnp.float32),
            pltpu.SemaphoreType.DMA((count, own_groups, len(at[0]))),
        ],
        input_output_aliases={2 + len(index) + len(flat) + owners: 0} if extra else {},
        compiler_params=pltpu.CompilerParams(vmem_limit_bytes=VMEM_LIMIT * MIB),
        cost_estimate=pl.CostEstimate(
            flops=(EARLY if keep else FULL) * count * here * owners * blocks * rows * slots * depth,
            bytes_accessed=4 * count * here * owners * blocks * rows,
            transcendentals=0,
        ),
        name="panel",
    )(place, green_occ, *index, *flat, *turned, *extra)


def after_kernel(token_ref, array_ref, out_ref):
    out_ref[...] = array_ref[...]


def after(token, array):
    vmem = pl.BlockSpec(memory_space=pltpu.VMEM)
    return pl.pallas_call(
        after_kernel,
        in_specs=[pl.BlockSpec(memory_space=pl.ANY), vmem],
        out_specs=vmem,
        out_shape=jax.ShapeDtypeStruct(array.shape, array.dtype),
        compiler_params=pltpu.CompilerParams(vmem_limit_bytes=4 * MIB),
        name="after",
    )(token, array)


def cycle(count):
    return list(range(0, count, 2)) + list(range(1, count, 2))[::-1]


def ring(count):
    walk = cycle(count)
    return [
        (2 * walk[n] + e, 2 * walk[(n + 1) % count] + e) for n in range(count) for e in range(2)
    ]


def swap(count):
    return [(n, n ^ 1) for n in range(count)]


def behind(index, steps, count):
    walk = cycle(count)
    return 2 * walk[(walk.index(index // 2) - steps) % count] + index % 2


def on_device(b3c_blocks, pair_index, green_occ, green_virt):
    per_device, slots, depth = b3c_blocks.shape
    blocks = pair_index.shape[0]
    rows = per_device // blocks
    n_row, n_col = lax.axis_size("row"), lax.axis_size("col")
    row, col = lax.axis_index("row"), lax.axis_index("col")
    outer, outer_row = n_col // 2, n_row // 2
    cuts = 2 if blocks % 2 == 0 else 1
    total = n_col * per_device
    groups = n_row * blocks // SUB
    split = 2 * blocks == SUB
    sizes = (blocks, slots, green_occ.shape[0], total, groups, per_device // cuts)
    raw = b3c_blocks.reshape(per_device * slots, depth)

    turn_col = functools.partial(lax.ppermute, axis_name="col", perm=ring(outer))
    swap_col = functools.partial(lax.ppermute, axis_name="col", perm=swap(n_col))
    turn_row = functools.partial(lax.ppermute, axis_name="row", perm=ring(outer_row))
    swap_row = functools.partial(lax.ppermute, axis_name="row", perm=swap(n_row))

    every = [(k, e, n) for k in range(outer) for e in range(2) for n in range(cuts)]
    number = {key: n_row + n for n, key in enumerate(every)}
    table = np.zeros((n_row, n_col, n_row + len(every)), np.int32)
    for r in range(n_row):
        for n in range(n_row):
            table[r, :, n] = behind(r, n // 2, outer_row) ^ (n % 2)
    for c in range(n_col):
        for key in every:
            k, e, cut = key
            table[:, c, number[key]] = (behind(c, k, outer) ^ e) * cuts + cut
    place = lax.dynamic_index_in_dim(
        jnp.asarray(table).reshape(n_row * n_col, -1), row * n_col + col, 0, keepdims=False
    )

    held, kept, state = {}, {}, {"panel": None}
    halves, turned = prepare(raw, pair_index, green_virt, cuts, rows)
    for n, piece in enumerate(halves):
        held[0, 0, n] = piece
    turned = [turned]
    for k in range(outer_row - 1):
        turned.append(turn_row(turned[-1]))
    paired = outer == 4 and cuts == 2 and split and outer_row == 2
    if not paired:
        turned = [a for t in turned for a in (t, swap_row(t))]
    index = [jnp.concatenate([pair_index, swap_row(pair_index)], axis=0)]
    for k in range(outer_row - 1):
        index.append(turn_row(index[-1]))

    def step(k, n):
        held[k, 0, n] = turn_col(held[k - 1, 0, n])

    def cross(k, n):
        held[k, 1, n] = swap_col(held[k, 0, n])

    def panel(units, first, count, keep=False, reuse=False, token=False):
        at = [[number[key] for key in unit] for unit in units]
        data = [[kept[tuple(unit)]] if reuse else [held[key] for key in unit] for unit in units]
        here = index[first // 2 : (first + count) // 2]
        state["panel"], *more = make_panel(
            place, green_occ, here, data, at, turned[first : first + count], first, sizes,
            state["panel"], keep, reuse, token,
        )
        if token:
            return more[0]
        for unit, array in zip(units, more):
            kept[tuple(unit)] = array

    if paired:
        A, B = 0, 1
        turned = [turned[0], swap_row(turned[0]), turned[1]]
        for n in range(2):
            step(1, n)
            cross(0, n)
            step(2, n)
        cross(1, A)
        early = [
            [(0, 0, A), (0, 0, B)], [(1, 0, A), (0, 1, A)], [(1, 0, B), (0, 1, B)]
        ]
        for unit in early[:2]:
            panel([unit], 0, 2, keep=True)
        turned.append(swap_row(turned[2]))
        panel(early[2:], 0, 2, keep=True)
        held[2, 0, A] = after(kept[tuple(early[2])], held[2, 0, A])
        step(3, A)
        cross(2, A)
        token = panel(early, 2, 2, reuse=True, token=True)
        held[2, 0, B] = after(token, held[2, 0, B])
        step(3, B)
        cross(2, B)
        token = panel([[(2, 0, A), (1, 1, A)]], 0, 4, token=True)
        held[3, 0, A] = after(token, held[3, 0, A])
        cross(3, A)
        held[1, 1, B] = turn_col(after(token, held[0, 1, B]))
        token = panel([[(2, 0, B), (2, 1, A)]], 0, 4, token=True)
        held[3, 0, B] = after(token, held[3, 0, B])
        cross(3, B)
        panel([[(3, 0, A), (2, 1, B)], [(3, 0, B), (3, 1, A)]], 0, 4)
        panel([[(1, 1, B), (3, 1, B)]], 0, 4)
    else:
        for k in range(outer):
            for n in range(cuts):
                if k > 0:
                    step(k, n)
                cross(k, n)
        for key in every:
            panel([[key]], 0, n_row)
    return state["panel"].reshape(total, n_row, 1, per_device)


def solution(mesh):
    return jax.shard_map(
        on_device,
        mesh=mesh,
        in_specs=(P(("row", "col"), None, None), P(("row", "col"), None), P(), P()),
        out_specs=P("row", None, "col", None),
        check_vma=False,
    )
```

```python
import functools

import jax
import jax.numpy as jnp
import numpy as np
from jax import lax
from jax.experimental import pallas as pl
from jax.experimental.pallas import tpu as pltpu
from jax.sharding import PartitionSpec as P

GROUP = 32
TAIL = 16
SUB = 8
MIB = 1 << 20
VMEM_LIMIT = 24
EARLY, FULL = 24, 18


def names_of(index_ref, first, count, lanes):
    slots = index_ref.shape[1]
    row = lax.broadcasted_iota(jnp.int32, (TAIL, lanes), 0)
    lane = lax.broadcasted_iota(jnp.int32, (TAIL, lanes), 1) % slots
    names = jnp.zeros((TAIL, lanes), jnp.float32)
    for b in range(count):
        for j in range(slots):
            here = (row == b) & (lane == j)
            names = jnp.where(here, index_ref[first + b, j].astype(jnp.float32), names)
    return names.astype(jnp.bfloat16)


def prepare_kernel(index_ref, raw_ref, virt_ref, *out_refs):
    *half_refs, turned_ref = out_refs
    depth = raw_ref.shape[1]
    blocks, slots = index_ref.shape
    rows = turned_ref.shape[1]
    per_piece = blocks // len(half_refs)
    span = raw_ref.shape[0] // len(half_refs)
    for n, half_ref in enumerate(half_refs):
        half = jnp.dot(
            raw_ref[n * span : (n + 1) * span, :], virt_ref[...], preferred_element_type=jnp.float32
        )
        half_ref[:span, :] = half.astype(jnp.bfloat16)
        half_ref[span:, :] = names_of(index_ref, n * per_piece, per_piece, depth)
    span = GROUP * slots
    to = lax.broadcasted_iota(jnp.int32, (span, span), 0)
    at = lax.broadcasted_iota(jnp.int32, (span, span), 1)
    same = (to // GROUP == at % slots) & (to % GROUP == at // slots)
    move = jnp.where(same, 1.0, 0.0).astype(jnp.bfloat16)
    for b in range(blocks):
        base = b * rows * slots
        parts = [
            jnp.dot(
                move,
                raw_ref[base + g * span : base + (g + 1) * span, :],
                preferred_element_type=jnp.float32,
            )
            for g in range(rows // GROUP)
        ]
        for j in range(slots):
            slab = jnp.concatenate([part[j * GROUP : (j + 1) * GROUP, :] for part in parts], axis=0)
            first = (b * slots + j) * depth
            turned_ref[first : first + depth, :] = slab.T.astype(jnp.bfloat16)


def prepare(raw, pair_index, green_virt, pieces, rows):
    span, depth = raw.shape[0] // pieces, raw.shape[1]
    blocks, slots = pair_index.shape
    vmem = pl.BlockSpec(memory_space=pltpu.VMEM)
    *halves, turned = pl.pallas_call(
        prepare_kernel,
        in_specs=[pl.BlockSpec(memory_space=pltpu.SMEM), vmem, vmem],
        out_specs=[vmem] * (pieces + 1),
        out_shape=[jax.ShapeDtypeStruct((span + TAIL, depth), jnp.bfloat16)] * pieces
        + [jax.ShapeDtypeStruct((blocks * slots * depth, rows), jnp.bfloat16)],
        compiler_params=pltpu.CompilerParams(vmem_limit_bytes=62 * MIB),
        name="prepare",
    )(pair_index, raw, green_virt)
    return halves, turned


def mix_pieces(occ_ref, piece_refs, mixed_ref, rows, slots):
    width, _, depth = mixed_ref.shape
    span = piece_refs[0].shape[0] - TAIL
    per_piece = span // (rows * slots)
    wide = GROUP * slots
    level = lax.broadcasted_iota(jnp.int32, (width, wide), 0).astype(jnp.float32)
    to = lax.broadcasted_iota(jnp.int32, (width * GROUP, wide), 0) % GROUP
    same = to == lax.broadcasted_iota(jnp.int32, (width * GROUP, wide), 1) // slots
    named = []
    for piece_ref in piece_refs:
        names = piece_ref[span:, :].astype(jnp.float32)
        for b in range(per_piece):
            name = jnp.concatenate([names[b : b + 1, :]] * (wide // depth), axis=1)
            named.append(jnp.where(level == name, 1.0, 0.0).astype(jnp.bfloat16))
    picked = lax.dot_general(
        occ_ref[...],
        jnp.concatenate(named, axis=1),
        (((0,), (0,)), ((), ())),
        preferred_element_type=jnp.float32,
    )
    for n, piece_ref in enumerate(piece_refs):
        for b in range(per_piece):
            at = (n * per_piece + b) * wide
            mix = jnp.broadcast_to(picked[:, None, at : at + wide], (width, GROUP, wide))
            mix = jnp.where(same, mix.reshape(width * GROUP, wide), 0.0).astype(jnp.bfloat16)
            base = b * rows * slots
            for g in range(0, rows // GROUP, 2):
                right = jnp.concatenate(
                    [
                        piece_ref[base + (g + e) * wide : base + (g + e + 1) * wide, :]
                        for e in range(2)
                    ],
                    axis=1,
                )
                part = jnp.dot(mix, right, preferred_element_type=jnp.float32).astype(jnp.bfloat16)
                for e in range(2):
                    first = (n * per_piece + b) * rows + (g + e) * GROUP
                    mixed_ref[:, first : first + GROUP, :] = part[
                        :, e * depth : (e + 1) * depth
                    ].reshape(width, GROUP, depth)


def panel_kernel(place_ref, occ_ref, *rest, plan):
    (units, kept, owners, extra, keep, token, blocks, slots, first_owner) = plan
    rest = list(rest)
    take = lambda count: [rest.pop(0) for _ in range(count)]
    index_refs = take(owners // 2)
    unit_refs = [take(1 if kept else len(unit)) for unit in units]
    turned_refs = take(owners)
    take(extra)
    out_ref = rest.pop(0)
    for token_ref in take(token):
        token_ref[0] = 0
    mixed_refs = [refs[0] for refs in unit_refs] if kept else take(len(units))
    out_buf, out_sem = rest
    here, depth = mixed_refs[0].shape[1:]
    height = here // len(units[0])
    per_group = SUB // blocks
    stores = []
    here_too = place_ref[0] >= 0
    for u, unit in enumerate(units):
        mixed_ref = mixed_refs[u]
        if not kept:

            @pl.when(here_too)
            def _():
                rows = turned_refs[0].shape[1]
                mix_pieces(occ_ref, unit_refs[u], mixed_ref, rows, slots)

        for g in range(owners // per_group):
            flat = out_buf.at[u, g].reshape((here + 1) * SUB, depth)
            tile = place_ref[first_owner + g * per_group] * blocks

            @pl.when(here_too)
            def _():
                for n in range(g * per_group, (g + 1) * per_group):
                    first = lax.rem(place_ref[first_owner + n] * blocks, SUB)
                    for b in range(blocks):
                        left = jnp.concatenate(
                            [
                                mixed_ref[index_refs[n // 2][n % 2 * blocks + b, j]]
                                for j in range(slots)
                            ],
                            axis=1,
                        )
                        right = turned_refs[n][b * slots * depth : (b + 1) * slots * depth, :]
                        flat[pl.ds(first + b, here, stride=SUB), :] = jnp.dot(
                            left, right, preferred_element_type=jnp.float32
                        )

            for n, at in enumerate(unit):
                first = pl.multiple_of(place_ref[at] * height, height)
                store = pltpu.make_async_copy(
                    out_buf.at[u, g, pl.ds(n * height, height)],
                    out_ref.at[pl.ds(first, height), tile // SUB],
                    out_sem.at[u, g, n],
                )
                store.start()
                stores.append(store)
    for store in stores:
        store.wait()


def make_panel(
    place, green_occ, index, units, at, turned, first_owner, sizes, before, keep, kept, token
):
    blocks, slots, width, total, groups, height = sizes
    depth, rows = turned[0].shape[0] // (blocks * slots), turned[0].shape[1]
    owners = len(turned)
    here = len(at[0]) * height
    own_groups = owners * blocks // SUB
    extra = [] if before is None else [before]
    flat = [a for unit in units for a in unit]
    plan = (at, kept, owners, len(extra), keep, token, blocks, slots, first_owner)
    anywhere = pl.BlockSpec(memory_space=pl.ANY)
    smem = pl.BlockSpec(memory_space=pltpu.SMEM)
    vmem = pl.BlockSpec(memory_space=pltpu.VMEM)
    mixed = jax.ShapeDtypeStruct((width, here, depth), jnp.bfloat16)
    out = jax.ShapeDtypeStruct((total, groups, SUB, depth), jnp.float32)
    count = len(units)
    return pl.pallas_call(
        functools.partial(panel_kernel, plan=plan),
        in_specs=[smem, vmem]
        + [smem] * len(index)
        + [vmem] * (len(flat) + owners)
        + [anywhere] * len(extra),
        out_specs=[anywhere] + [smem] * token + [vmem] * (count * keep),
        out_shape=[out]
        + [jax.ShapeDtypeStruct((1,), jnp.int32)] * token
        + [mixed] * (count * keep),
        scratch_shapes=[pltpu.VMEM(mixed.shape, mixed.dtype)] * (0 if keep or kept else count)
        + [
            pltpu.VMEM((count, own_groups, here + 1, SUB, depth), jnp.float32),
            pltpu.SemaphoreType.DMA((count, own_groups, len(at[0]))),
        ],
        input_output_aliases={2 + len(index) + len(flat) + owners: 0} if extra else {},
        compiler_params=pltpu.CompilerParams(vmem_limit_bytes=VMEM_LIMIT * MIB),
        cost_estimate=pl.CostEstimate(
            flops=(EARLY if keep else FULL) * count * here * owners * blocks * rows * slots * depth,
            bytes_accessed=4 * count * here * owners * blocks * rows,
            transcendentals=0,
        ),
        name="panel",
    )(place, green_occ, *index, *flat, *turned, *extra)


def after_kernel(token_ref, array_ref, out_ref):
    out_ref[...] = array_ref[...]


def after(token, array):
    vmem = pl.BlockSpec(memory_space=pltpu.VMEM)
    return pl.pallas_call(
        after_kernel,
        in_specs=[pl.BlockSpec(memory_space=pl.ANY), vmem],
        out_specs=vmem,
        out_shape=jax.ShapeDtypeStruct(array.shape, array.dtype),
        compiler_params=pltpu.CompilerParams(vmem_limit_bytes=4 * MIB),
        name="after",
    )(token, array)


def cycle(count):
    return list(range(0, count, 2)) + list(range(1, count, 2))[::-1]


def ring(count):
    walk = cycle(count)
    return [
        (2 * walk[n] + e, 2 * walk[(n + 1) % count] + e) for n in range(count) for e in range(2)
    ]


def swap(count):
    return [(n, n ^ 1) for n in range(count)]


def behind(index, steps, count):
    walk = cycle(count)
    return 2 * walk[(walk.index(index // 2) - steps) % count] + index % 2


def on_device(b3c_blocks, pair_index, green_occ, green_virt):
    per_device, slots, depth = b3c_blocks.shape
    blocks = pair_index.shape[0]
    rows = per_device // blocks
    n_row, n_col = lax.axis_size("row"), lax.axis_size("col")
    row, col = lax.axis_index("row"), lax.axis_index("col")
    outer, outer_row = n_col // 2, n_row // 2
    cuts = 2 if blocks % 2 == 0 else 1
    total = n_col * per_device
    groups = n_row * blocks // SUB
    split = 2 * blocks == SUB
    sizes = (blocks, slots, green_occ.shape[0], total, groups, per_device // cuts)
    raw = b3c_blocks.reshape(per_device * slots, depth)

    turn_col = functools.partial(lax.ppermute, axis_name="col", perm=ring(outer))
    swap_col = functools.partial(lax.ppermute, axis_name="col", perm=swap(n_col))
    turn_row = functools.partial(lax.ppermute, axis_name="row", perm=ring(outer_row))
    swap_row = functools.partial(lax.ppermute, axis_name="row", perm=swap(n_row))

    every = [(k, e, n) for k in range(outer) for e in range(2) for n in range(cuts)]
    number = {key: n_row + n for n, key in enumerate(every)}
    table = np.zeros((n_row, n_col, n_row + len(every)), np.int32)
    for r in range(n_row):
        for n in range(n_row):
            table[r, :, n] = behind(r, n // 2, outer_row) ^ (n % 2)
    for c in range(n_col):
        for key in every:
            k, e, cut = key
            table[:, c, number[key]] = (behind(c, k, outer) ^ e) * cuts + cut
    place = lax.dynamic_index_in_dim(
        jnp.asarray(table).reshape(n_row * n_col, -1), row * n_col + col, 0, keepdims=False
    )

    held, kept, state = {}, {}, {"panel": None}
    halves, turned = prepare(raw, pair_index, green_virt, cuts, rows)
    for n, piece in enumerate(halves):
        held[0, 0, n] = piece
    turned = [turned]
    for k in range(outer_row - 1):
        turned.append(turn_row(turned[-1]))
    paired = outer == 4 and cuts == 2 and split and outer_row == 2
    if not paired:
        turned = [a for t in turned for a in (t, swap_row(t))]
    index = [jnp.concatenate([pair_index, swap_row(pair_index)], axis=0)]
    for k in range(outer_row - 1):
        index.append(turn_row(index[-1]))

    def step(k, n):
        held[k, 0, n] = turn_col(held[k - 1, 0, n])

    def cross(k, n):
        held[k, 1, n] = swap_col(held[k, 0, n])

    def panel(units, first, count, keep=False, reuse=False, token=False):
        at = [[number[key] for key in unit] for unit in units]
        data = [[kept[tuple(unit)]] if reuse else [held[key] for key in unit] for unit in units]
        here = index[first // 2 : (first + count) // 2]
        state["panel"], *more = make_panel(
            place, green_occ, here, data, at, turned[first : first + count], first, sizes,
            state["panel"], keep, reuse, token,
        )
        if token:
            return more[0]
        for unit, array in zip(units, more):
            kept[tuple(unit)] = array

    if paired:
        A, B = 0, 1
        turned = [turned[0], swap_row(turned[0]), turned[1]]
        for n in range(2):
            step(1, n)
            cross(0, n)
            step(2, n)
        cross(1, A)
        early = [
            [(0, 0, A), (0, 0, B)], [(1, 0, A), (0, 1, A)], [(1, 0, B), (0, 1, B)]
        ]
        for unit in early[:2]:
            panel([unit], 0, 2, keep=True)
        turned.append(swap_row(turned[2]))
        panel(early[2:], 0, 2, keep=True)
        held[2, 0, A] = after(kept[tuple(early[2])], held[2, 0, A])
        step(3, A)
        cross(2, A)
        token = panel(early, 2, 2, reuse=True, token=True)
        held[2, 0, B] = after(token, held[2, 0, B])
        step(3, B)
        cross(2, B)
        token = panel([[(2, 0, A), (1, 1, A)]], 0, 4, token=True)
        held[3, 0, A] = after(token, held[3, 0, A])
        cross(3, A)
        held[1, 1, B] = turn_col(after(token, held[0, 1, B]))
        token = panel([[(2, 0, B), (2, 1, A)]], 0, 4, token=True)
        held[3, 0, B] = after(token, held[3, 0, B])
        cross(3, B)
        panel([[(3, 0, A), (2, 1, B)], [(3, 0, B), (3, 1, A)]], 0, 4)
        panel([[(1, 1, B), (3, 1, B)]], 0, 4)
    else:
        for k in range(outer):
            for n in range(cuts):
                if k > 0:
                    step(k, n)
                cross(k, n)
        for key in every:
            panel([[key]], 0, n_row)
    return state["panel"].reshape(total, n_row, 1, per_device)


def solution(mesh):
    return jax.shard_map(
        on_device,
        mesh=mesh,
        in_specs=(P(("row", "col"), None, None), P(("row", "col"), None), P(), P()),
        out_specs=P("row", None, "col", None),
        check_vma=False,
    )
```

```python
import functools

import jax
import jax.numpy as jnp
import numpy as np
from jax import lax
from jax.experimental import pallas as pl
from jax.experimental.pallas import tpu as pltpu
from jax.sharding import PartitionSpec as P

GROUP = 32
TAIL = 16
SUB = 8
MIB = 1 << 20
VMEM_LIMIT = 24
EARLY, FULL = 24, 18


def names_of(index_ref, first, count, lanes):
    slots = index_ref.shape[1]
    row = lax.broadcasted_iota(jnp.int32, (TAIL, lanes), 0)
    lane = lax.broadcasted_iota(jnp.int32, (TAIL, lanes), 1) % slots
    names = jnp.zeros((TAIL, lanes), jnp.float32)
    for b in range(count):
        for j in range(slots):
            here = (row == b) & (lane == j)
            names = jnp.where(here, index_ref[first + b, j].astype(jnp.float32), names)
    return names.astype(jnp.bfloat16)


def prepare_kernel(index_ref, raw_ref, virt_ref, *out_refs):
    *half_refs, turned_ref = out_refs
    depth = raw_ref.shape[1]
    blocks, slots = index_ref.shape
    rows = turned_ref.shape[1]
    per_piece = blocks // len(half_refs)
    span = raw_ref.shape[0] // len(half_refs)
    for n, half_ref in enumerate(half_refs):
        half = jnp.dot(
            raw_ref[n * span : (n + 1) * span, :], virt_ref[...], preferred_element_type=jnp.float32
        )
        half_ref[:span, :] = half.astype(jnp.bfloat16)
        half_ref[span:, :] = names_of(index_ref, n * per_piece, per_piece, depth)
    span = GROUP * slots
    to = lax.broadcasted_iota(jnp.int32, (span, span), 0)
    at = lax.broadcasted_iota(jnp.int32, (span, span), 1)
    same = (to // GROUP == at % slots) & (to % GROUP == at // slots)
    move = jnp.where(same, 1.0, 0.0).astype(jnp.bfloat16)
    for b in range(blocks):
        base = b * rows * slots
        parts = [
            jnp.dot(
                move,
                raw_ref[base + g * span : base + (g + 1) * span, :],
                preferred_element_type=jnp.float32,
            )
            for g in range(rows // GROUP)
        ]
        for j in range(slots):
            slab = jnp.concatenate([part[j * GROUP : (j + 1) * GROUP, :] for part in parts], axis=0)
            first = (b * slots + j) * depth
            turned_ref[first : first + depth, :] = slab.T.astype(jnp.bfloat16)


def prepare(raw, pair_index, green_virt, pieces, rows):
    span, depth = raw.shape[0] // pieces, raw.shape[1]
    blocks, slots = pair_index.shape
    vmem = pl.BlockSpec(memory_space=pltpu.VMEM)
    *halves, turned = pl.pallas_call(
        prepare_kernel,
        in_specs=[pl.BlockSpec(memory_space=pltpu.SMEM), vmem, vmem],
        out_specs=[vmem] * (pieces + 1),
        out_shape=[jax.ShapeDtypeStruct((span + TAIL, depth), jnp.bfloat16)] * pieces
        + [jax.ShapeDtypeStruct((blocks * slots * depth, rows), jnp.bfloat16)],
        compiler_params=pltpu.CompilerParams(vmem_limit_bytes=62 * MIB),
        name="prepare",
    )(pair_index, raw, green_virt)
    return halves, turned


def mix_pieces(occ_ref, piece_refs, mixed_ref, rows, slots):
    width, _, depth = mixed_ref.shape
    span = piece_refs[0].shape[0] - TAIL
    per_piece = span // (rows * slots)
    wide = GROUP * slots
    level = lax.broadcasted_iota(jnp.int32, (width, wide), 0).astype(jnp.float32)
    to = lax.broadcasted_iota(jnp.int32, (width * GROUP, wide), 0) % GROUP
    same = to == lax.broadcasted_iota(jnp.int32, (width * GROUP, wide), 1) // slots
    named = []
    for piece_ref in piece_refs:
        names = piece_ref[span:, :].astype(jnp.float32)
        for b in range(per_piece):
            name = jnp.concatenate([names[b : b + 1, :]] * (wide // depth), axis=1)
            named.append(jnp.where(level == name, 1.0, 0.0).astype(jnp.bfloat16))
    picked = lax.dot_general(
        occ_ref[...],
        jnp.concatenate(named, axis=1),
        (((0,), (0,)), ((), ())),
        preferred_element_type=jnp.float32,
    )
    for n, piece_ref in enumerate(piece_refs):
        for b in range(per_piece):
            at = (n * per_piece + b) * wide
            mix = jnp.broadcast_to(picked[:, None, at : at + wide], (width, GROUP, wide))
            mix = jnp.where(same, mix.reshape(width * GROUP, wide), 0.0).astype(jnp.bfloat16)
            base = b * rows * slots
            for g in range(0, rows // GROUP, 2):
                right = jnp.concatenate(
                    [
                        piece_ref[base + (g + e) * wide : base + (g + e + 1) * wide, :]
                        for e in range(2)
                    ],
                    axis=1,
                )
                part = jnp.dot(mix, right, preferred_element_type=jnp.float32).astype(jnp.bfloat16)
                for e in range(2):
                    first = (n * per_piece + b) * rows + (g + e) * GROUP
                    mixed_ref[:, first : first + GROUP, :] = part[
                        :, e * depth : (e + 1) * depth
                    ].reshape(width, GROUP, depth)


def panel_kernel(place_ref, occ_ref, *rest, plan):
    (units, kept, owners, extra, keep, token, blocks, slots, first_owner) = plan
    rest = list(rest)
    take = lambda count: [rest.pop(0) for _ in range(count)]
    index_refs = take(owners // 2)
    unit_refs = [take(1 if kept else len(unit)) for unit in units]
    turned_refs = take(owners)
    take(extra)
    out_ref = rest.pop(0)
    for token_ref in take(token):
        token_ref[0] = 0
    mixed_refs = [refs[0] for refs in unit_refs] if kept else take(len(units))
    out_buf, out_sem = rest
    here, depth = mixed_refs[0].shape[1:]
    height = here // len(units[0])
    per_group = SUB // blocks
    stores = []
    here_too = place_ref[0] >= 0
    for u, unit in enumerate(units):
        mixed_ref = mixed_refs[u]
        if not kept:

            @pl.when(here_too)
            def _():
                rows = turned_refs[0].shape[1]
                mix_pieces(occ_ref, unit_refs[u], mixed_ref, rows, slots)

        for g in range(owners // per_group):
            flat = out_buf.at[u, g].reshape((here + 1) * SUB, depth)
            tile = place_ref[first_owner + g * per_group] * blocks

            @pl.when(here_too)
            def _():
                for n in range(g * per_group, (g + 1) * per_group):
                    first = lax.rem(place_ref[first_owner + n] * blocks, SUB)
                    for b in range(blocks):
                        left = jnp.concatenate(
                            [
                                mixed_ref[index_refs[n // 2][n % 2 * blocks + b, j]]
                                for j in range(slots)
                            ],
                            axis=1,
                        )
                        right = turned_refs[n][b * slots * depth : (b + 1) * slots * depth, :]
                        flat[pl.ds(first + b, here, stride=SUB), :] = jnp.dot(
                            left, right, preferred_element_type=jnp.float32
                        )

            for n, at in enumerate(unit):
                first = pl.multiple_of(place_ref[at] * height, height)
                store = pltpu.make_async_copy(
                    out_buf.at[u, g, pl.ds(n * height, height)],
                    out_ref.at[pl.ds(first, height), tile // SUB],
                    out_sem.at[u, g, n],
                )
                store.start()
                stores.append(store)
    for store in stores:
        store.wait()


def make_panel(
    place, green_occ, index, units, at, turned, first_owner, sizes, before, keep, kept, token
):
    blocks, slots, width, total, groups, height = sizes
    depth, rows = turned[0].shape[0] // (blocks * slots), turned[0].shape[1]
    owners = len(turned)
    here = len(at[0]) * height
    own_groups = owners * blocks // SUB
    extra = [] if before is None else [before]
    flat = [a for unit in units for a in unit]
    plan = (at, kept, owners, len(extra), keep, token, blocks, slots, first_owner)
    anywhere = pl.BlockSpec(memory_space=pl.ANY)
    smem = pl.BlockSpec(memory_space=pltpu.SMEM)
    vmem = pl.BlockSpec(memory_space=pltpu.VMEM)
    mixed = jax.ShapeDtypeStruct((width, here, depth), jnp.bfloat16)
    out = jax.ShapeDtypeStruct((total, groups, SUB, depth), jnp.float32)
    count = len(units)
    return pl.pallas_call(
        functools.partial(panel_kernel, plan=plan),
        in_specs=[smem, vmem]
        + [smem] * len(index)
        + [vmem] * (len(flat) + owners)
        + [anywhere] * len(extra),
        out_specs=[anywhere] + [smem] * token + [vmem] * (count * keep),
        out_shape=[out]
        + [jax.ShapeDtypeStruct((1,), jnp.int32)] * token
        + [mixed] * (count * keep),
        scratch_shapes=[pltpu.VMEM(mixed.shape, mixed.dtype)] * (0 if keep or kept else count)
        + [
            pltpu.VMEM((count, own_groups, here + 1, SUB, depth), jnp.float32),
            pltpu.SemaphoreType.DMA((count, own_groups, len(at[0]))),
        ],
        input_output_aliases={2 + len(index) + len(flat) + owners: 0} if extra else {},
        compiler_params=pltpu.CompilerParams(vmem_limit_bytes=VMEM_LIMIT * MIB),
        cost_estimate=pl.CostEstimate(
            flops=(EARLY if keep else FULL) * count * here * owners * blocks * rows * slots * depth,
            bytes_accessed=4 * count * here * owners * blocks * rows,
            transcendentals=0,
        ),
        name="panel",
    )(place, green_occ, *index, *flat, *turned, *extra)


def after_kernel(token_ref, *refs):
    count = len(refs) // 2
    for array_ref, out_ref in zip(refs[:count], refs[count:]):
        out_ref[...] = array_ref[...]


def after(token, *arrays):
    vmem = pl.BlockSpec(memory_space=pltpu.VMEM)
    return pl.pallas_call(
        after_kernel,
        in_specs=[pl.BlockSpec(memory_space=pl.ANY)] + [vmem] * len(arrays),
        out_specs=[vmem] * len(arrays),
        out_shape=[jax.ShapeDtypeStruct(a.shape, a.dtype) for a in arrays],
        compiler_params=pltpu.CompilerParams(vmem_limit_bytes=4 * MIB),
        name="after",
    )(token, *arrays)


def cycle(count):
    return list(range(0, count, 2)) + list(range(1, count, 2))[::-1]


def ring(count):
    walk = cycle(count)
    return [
        (2 * walk[n] + e, 2 * walk[(n + 1) % count] + e) for n in range(count) for e in range(2)
    ]


def swap(count):
    return [(n, n ^ 1) for n in range(count)]


def behind(index, steps, count):
    walk = cycle(count)
    return 2 * walk[(walk.index(index // 2) - steps) % count] + index % 2


def on_device(b3c_blocks, pair_index, green_occ, green_virt):
    per_device, slots, depth = b3c_blocks.shape
    blocks = pair_index.shape[0]
    rows = per_device // blocks
    n_row, n_col = lax.axis_size("row"), lax.axis_size("col")
    row, col = lax.axis_index("row"), lax.axis_index("col")
    outer, outer_row = n_col // 2, n_row // 2
    cuts = 2 if blocks % 2 == 0 else 1
    total = n_col * per_device
    groups = n_row * blocks // SUB
    split = 2 * blocks == SUB
    sizes = (blocks, slots, green_occ.shape[0], total, groups, per_device // cuts)
    raw = b3c_blocks.reshape(per_device * slots, depth)

    turn_col = functools.partial(lax.ppermute, axis_name="col", perm=ring(outer))
    swap_col = functools.partial(lax.ppermute, axis_name="col", perm=swap(n_col))
    turn_row = functools.partial(lax.ppermute, axis_name="row", perm=ring(outer_row))
    swap_row = functools.partial(lax.ppermute, axis_name="row", perm=swap(n_row))

    every = [(k, e, n) for k in range(outer) for e in range(2) for n in range(cuts)]
    number = {key: n_row + n for n, key in enumerate(every)}
    table = np.zeros((n_row, n_col, n_row + len(every)), np.int32)
    for r in range(n_row):
        for n in range(n_row):
            table[r, :, n] = behind(r, n // 2, outer_row) ^ (n % 2)
    for c in range(n_col):
        for key in every:
            k, e, cut = key
            table[:, c, number[key]] = (behind(c, k, outer) ^ e) * cuts + cut
    place = lax.dynamic_index_in_dim(
        jnp.asarray(table).reshape(n_row * n_col, -1), row * n_col + col, 0, keepdims=False
    )

    held, kept, state = {}, {}, {"panel": None}
    halves, turned = prepare(raw, pair_index, green_virt, cuts, rows)
    for n, piece in enumerate(halves):
        held[0, 0, n] = piece
    turned = [turned]
    for k in range(outer_row - 1):
        turned.append(turn_row(turned[-1]))
    paired = outer == 4 and cuts == 2 and split and outer_row == 2
    if not paired:
        turned = [a for t in turned for a in (t, swap_row(t))]
    index = [jnp.concatenate([pair_index, swap_row(pair_index)], axis=0)]
    for k in range(outer_row - 1):
        index.append(turn_row(index[-1]))

    def step(k, n):
        held[k, 0, n] = turn_col(held[k - 1, 0, n])

    def cross(k, n):
        held[k, 1, n] = swap_col(held[k, 0, n])

    def panel(units, first, count, keep=False, reuse=False, token=False):
        at = [[number[key] for key in unit] for unit in units]
        data = [[kept[tuple(unit)]] if reuse else [held[key] for key in unit] for unit in units]
        here = index[first // 2 : (first + count) // 2]
        state["panel"], *more = make_panel(
            place, green_occ, here, data, at, turned[first : first + count], first, sizes,
            state["panel"], keep, reuse, token,
        )
        if token:
            return more[0]
        for unit, array in zip(units, more):
            kept[tuple(unit)] = array

    if paired:
        A, B = 0, 1
        turned = [turned[0], swap_row(turned[0]), turned[1]]
        for n in range(2):
            step(1, n)
            cross(0, n)
            step(2, n)
        cross(1, A)
        early = [
            [(0, 0, A), (0, 0, B)], [(1, 0, A), (0, 1, A)], [(1, 0, B), (0, 1, B)]
        ]
        for unit in early[:2]:
            panel([unit], 0, 2, keep=True)
        turned.append(swap_row(turned[2]))
        panel(early[2:], 0, 2, keep=True)
        (held[2, 0, A],) = after(kept[tuple(early[2])], held[2, 0, A])
        step(3, A)
        cross(2, A)
        token = panel(early, 2, 2, reuse=True, token=True)
        (held[2, 0, B],) = after(token, held[2, 0, B])
        step(3, B)
        cross(2, B)
        token = panel([[(2, 0, A), (1, 1, A)]], 0, 4, token=True)
        held[3, 0, A], late = after(token, held[3, 0, A], held[0, 1, B])
        cross(3, A)
        held[1, 1, B] = turn_col(late)
        token = panel([[(2, 0, B), (2, 1, A)]], 0, 4, token=True)
        (held[3, 0, B],) = after(token, held[3, 0, B])
        cross(3, B)
        panel([[(3, 0, A), (2, 1, B)], [(3, 0, B), (3, 1, A)]], 0, 4)
        panel([[(1, 1, B), (3, 1, B)]], 0, 4)
    else:
        for k in range(outer):
            for n in range(cuts):
                if k > 0:
                    step(k, n)
                cross(k, n)
        for key in every:
            panel([[key]], 0, n_row)
    return state["panel"].reshape(total, n_row, 1, per_device)


def solution(mesh):
    return jax.shard_map(
        on_device,
        mesh=mesh,
        in_specs=(P(("row", "col"), None, None), P(("row", "col"), None), P(), P()),
        out_specs=P("row", None, "col", None),
        check_vma=False,
    )
```
